512 devices in a mesh: replica: 32 (over y, z_hi, core), tensor: 16 (over z_lo, x).
Axes of the slice: x: 4, y: 8, z: 8 (z_hi: 2, z_lo: 4; z = z_hi * 4 + z_lo), core: 2. Of those that a mesh axis runs over, the one named last changes fastest.
Arguments:
- trainer_weight: bfloat16 [5120, 2048], P(('replica', 'tensor')), may hold values from -0.25 to 0.25
- hidden_new: bfloat16 [512, 5120], P('replica'), may hold values from -6 to 6
- queries: bfloat16 [512, 8192], P('replica', 'tensor'), may hold values from -130 to 130
- key_cache: int32 [512, 16, 128, 128], P('replica', 'tensor'), may hold values from -128 to 127
- key_scales: float32 [512, 16, 128], P('replica', 'tensor'), may hold values from 0.005 to 0.02
- value_cache: int32 [512, 16, 128, 128], P('replica', 'tensor'), may hold values from -128 to 127
- value_scales: float32 [512, 16, 128], P('replica', 'tensor'), may hold values from 0.005 to 0.05
- lengths: int32 [512], P('replica'), may hold values from 1 to 256
Outputs:
- synced: bfloat16 [5120, 2048], P(None, 'tensor')
- block_scales: float32 [40, 16], P(None, 'tensor')
- attended: bfloat16 [512, 8192], P('replica', 'tensor')
The draws below stay inside these ranges and needn't reach their ends.
All inputs are finite; a program needn't handle non-finite values.
Results may differ from the reference program's by a relative error of at most 0.0021.
Values may be sent and summed in bfloat16 or wider, within the bound.
A program may use at most 64 MiB of HBM per device.

```python
import math
import jax
import jax.numpy as jnp
from jax import lax

D = 5120
HD = 128
GROUP = 8
QB = 128
CTXH = 128
KVH = 8
QH = 64
C = 2048
ROWS = 512


def cache_draw(key):
    entries = jax.random.randint(jax.random.fold_in(key, 11), (ROWS, 2 * KVH, CTXH, HD), -128, 128, dtype=jnp.int32)
    logs = jax.random.uniform(jax.random.fold_in(key, 12), (ROWS, 2 * KVH, CTXH), jnp.float32, math.log(0.005), math.log(0.02))
    return (entries, jnp.exp(logs))


def draw_key_cache(key, part):
    entries, scales = cache_draw(key)
    return entries


def draw_key_scales(key, part):
    entries, scales = cache_draw(key)
    return scales.astype(jnp.float32)


def draw_queries(key, part):
    key = jax.random.fold_in(key, 3)
    first = jax.random.fold_in(key, 0)
    result = jnp.clip(jax.random.normal(first, (ROWS, QH * HD), jnp.float32), -6.0, 6.0)
    return result.astype(jnp.bfloat16)


def draw_trainer_weight(key, part):
    key = jax.random.fold_in(key, 5)
    first, second, third = jax.random.split(key, 3)
    row_scale = jnp.exp(jax.random.uniform(first, (D, 1), jnp.float32, 0.0, math.log(10.0)))
    column_scale = jnp.exp(jax.random.uniform(second, (1, C), jnp.float32, 0.0, math.log(10.0)))
    core = jnp.clip(jax.random.normal(third, (D, C), jnp.float32), -5.0, 5.0)
    scaled = core * row_scale * column_scale / (30.0 * math.sqrt(D))
    return jnp.clip(scaled, -0.25, 0.25).astype(jnp.bfloat16)


def draw_lengths(key, part):
    key = jax.random.fold_in(key, 7)
    drawn = jax.random.randint(key, (ROWS,), 1, 2 * CTXH + 1, dtype=jnp.int32)
    return drawn.at[0].set(2 * CTXH)


def with_ends(result, own_key, smallest, top_value):
    place = [jax.random.randint(jax.random.fold_in(own_key, axis), (), 0, length) for axis, length in enumerate(result.shape)]
    main_axis = result.shape.index(max(result.shape))
    neighbour = place[:main_axis] + [(place[main_axis] + 1) % result.shape[main_axis]] + place[main_axis + 1:]
    return result.at[tuple(place)].set(smallest).at[tuple(neighbour)].set(top_value)


def levels(stream_key, dims, shards, low, high):
    gain = 1.0
    for dim, blocks in shards:
        steps = jax.random.uniform(jax.random.fold_in(jax.random.fold_in(stream_key, 6), dim), (blocks,), jnp.float32, low / len(shards), high / len(shards))
        gain = gain * jnp.repeat(jnp.exp(steps), dims[dim] // blocks).reshape((-1,) + (1,) * (len(dims) - 1 - dim))
    return gain


def gaussian(stream_key, extent, spread, limit, cuts=(), kind=jnp.bfloat16):
    array = spread * jax.random.normal(stream_key, extent, jnp.float32)
    if cuts:
        array = array * levels(stream_key, extent, cuts, -0.22, 0.18)
    return jnp.clip(array, -limit, limit).astype(kind)


def setup_inputs(seed: int = 0) -> dict:
    keys = jax.random.split(jax.random.key(seed), 9)
    trainer_weight = draw_trainer_weight(jax.random.fold_in(keys[8], 71), 0)
    hidden_new = gaussian(keys[1], (ROWS, D), 1.0, 6.0, ((0, 32),))
    queries = draw_queries(jax.random.fold_in(keys[8], 71), 0)
    key_cache = draw_key_cache(jax.random.fold_in(keys[8], 71), 0)
    key_scales = draw_key_scales(jax.random.fold_in(keys[8], 71), 0)
    value_cache = with_ends(jax.random.randint(keys[5], (ROWS, 2 * KVH, CTXH, HD), -128, 128), jax.random.fold_in(keys[5], 1), -128, 127).astype(jnp.int32)
    value_scales = jnp.clip(jnp.exp(math.log(0.05) - 2.3025851 * jax.random.uniform(keys[6], (ROWS, 2 * KVH, CTXH), jnp.float32) ** levels(keys[6], (ROWS, 2 * KVH, CTXH), ((0, 32), (1, 16)), -0.2, 0.2)), 0.005, 0.05)
    lengths = draw_lengths(jax.random.fold_in(keys[8], 71), 0)
    return dict(trainer_weight=trainer_weight, hidden_new=hidden_new, queries=queries, key_cache=key_cache, key_scales=key_scales, value_cache=value_cache, value_scales=value_scales, lengths=lengths)


EPSILON = 1e-06
ROPE_BASE = 1000000.0
MASKED = -1e+30

def frequencies(head_dim):
    return ROPE_BASE ** (-(jnp.arange(head_dim // 2, dtype=jnp.float32) * 2.0 / head_dim))

def rotate(vectors, angles):
    half_width = vectors.shape[-1] // 2
    cosine = jnp.cos(angles)
    sine = jnp.sin(angles)
    first = vectors[..., :half_width]
    second = vectors[..., half_width:]
    return jnp.concatenate([first * cosine - second * sine, second * cosine + first * sine], axis=-1)

def reference(trainer_weight, hidden_new, queries, key_cache, key_scales, value_cache, value_scales, lengths):
    blocks_r = D // QB
    blocks_c = C // QB
    weight32 = trainer_weight.astype(jnp.float32)
    magnitude = jnp.abs(weight32).reshape(blocks_r, QB, blocks_c, QB)
    block_scales = lax.optimization_barrier(jnp.max(magnitude, axis=(1, 3))) + EPSILON
    synced = (weight32.reshape(blocks_r, QB, blocks_c, QB) / block_scales[:, None, :, None]).reshape(D, C).astype(jnp.bfloat16)
    total_rows = hidden_new.shape[0]
    partial_value = jnp.einsum('rbi,bic->rbc', hidden_new.astype(jnp.float32).reshape(total_rows, blocks_r, QB), synced.astype(jnp.float32).reshape(blocks_r, QB, C), precision=lax.Precision.HIGHEST)
    column_scales = jnp.repeat(block_scales, QB, axis=1)
    projected = lax.optimization_barrier(jnp.sum(partial_value * column_scales[None], axis=1)).reshape(total_rows, KVH, 2, HD)
    angles = lengths.astype(jnp.float32)[:, None, None] * frequencies(HD)
    keys_new = rotate(projected[:, :, 0, :], angles).astype(jnp.bfloat16)
    values_new = projected[:, :, 1, :].astype(jnp.bfloat16)
    grouped = queries.reshape(total_rows, KVH, GROUP, HD)
    position = jnp.arange(2 * CTXH, dtype=jnp.int32)
    live_mask = (position[None, :] < lengths[:, None]).astype(jnp.float32)
    root = math.sqrt(HD)

    def one_head(kv_head):
        query_rows = lax.dynamic_index_in_dim(grouped, kv_head, 1, keepdims=False).astype(jnp.float32)
        first = (2 * kv_head).astype(jnp.int32)
        key_ints = lax.dynamic_slice_in_dim(key_cache, first, 2, 1).reshape(total_rows, 2 * CTXH, HD)
        key_scale = lax.dynamic_slice_in_dim(key_scales, first, 2, 1).reshape(total_rows, 2 * CTXH)
        key_rows = key_ints.astype(jnp.float32) * key_scale[:, :, None]
        value_ints = lax.dynamic_slice_in_dim(value_cache, first, 2, 1).reshape(total_rows, 2 * CTXH, HD)
        value_scale = lax.dynamic_slice_in_dim(value_scales, first, 2, 1).reshape(total_rows, 2 * CTXH)
        value_rows = value_ints.astype(jnp.float32) * value_scale[:, :, None]
        key_fresh = lax.dynamic_index_in_dim(keys_new, kv_head, 1, keepdims=False).astype(jnp.float32)
        value_fresh = lax.dynamic_index_in_dim(values_new, kv_head, 1, keepdims=False).astype(jnp.float32)
        scores = jnp.einsum('rjd,rpd->rjp', query_rows, key_rows, precision=lax.Precision.HIGHEST) / root
        scores = jnp.where(live_mask[:, None, :] > 0.5, scores, MASKED)
        fresh_score = jnp.einsum('rjd,rd->rj', query_rows, key_fresh, precision=lax.Precision.HIGHEST) / root
        row_peak = jnp.maximum(lax.optimization_barrier(jnp.max(scores, axis=-1)), fresh_score)
        weights = jnp.exp(scores - row_peak[..., None]) * live_mask[:, None, :]
        fresh_weight = jnp.exp(fresh_score - row_peak)
        weight_sum = lax.optimization_barrier(jnp.sum(weights, axis=-1)) + fresh_weight
        weighted = jnp.einsum('rjp,rpd->rjd', weights, value_rows, precision=lax.Precision.HIGHEST)
        weighted = weighted + fresh_weight[..., None] * value_fresh[:, None, :]
        return weighted / weight_sum[..., None]
    per_head = lax.map(one_head, jnp.arange(KVH, dtype=jnp.int32))
    attended = jnp.transpose(per_head, (1, 0, 2, 3)).reshape(total_rows, QH * HD).astype(jnp.bfloat16)
    return (synced, block_scales, attended)
```

```python
import math

import jax
import jax.numpy as jnp
from jax import lax
from jax.experimental import pallas as pl
from jax.experimental.pallas import tpu as pltpu
from jax.sharding import PartitionSpec as P

HEADS = 4
QB = 128
EPSILON = 1e-06
ROPE_BASE = 1000000.0
MASKED = -1e30
MESH = pl.DeviceIdType.MESH

NY = 8
PLANE = 32
TENSORS = 16


def kernel(
    w_hbm, hid_hbm, q_hbm, kc_hbm, ks_hbm, vc_hbm, vs_hbm, len_hbm,
    synced_out, scale_out, att_out,
    w_v, hid_v, q_v, pq_v, kc_v, ks_v, vc_v, vs_v, len_s,
    stage, landed, packed, gathered, scale_v,
    qs, osc, mlsc, psend, precv, esend, erecv,
    load_sem, a_send, a_recv, ring_send, ring_recv, sib_send, sib_recv,
    pair_send, pair_recv,
):
    rep = lax.axis_index("replica")
    ten = lax.axis_index("tensor")
    y = rep // 4
    zhi = (rep // 2) % 2
    core = rep % 2
    me = zhi * TENSORS + ten
    half = ten % 2

    def replica_of(yy, zz, cc):
        return (yy * 2 + zz) * 2 + cc

    def plane_id(s):
        return {"replica": replica_of(y, s // TENSORS, core), "tensor": s % TENSORS}

    up = (y + 1) % NY
    down = (y + NY - 1) % NY
    up_id = {"replica": replica_of(up, zhi, core), "tensor": ten}
    down_id = {"replica": replica_of(down, zhi, core), "tensor": ten}
    sib_id = {"replica": replica_of(y, zhi, 1 - core), "tensor": ten}
    pair_id = {"replica": rep, "tensor": ten + 1 - 2 * half}

    barrier = pltpu.get_barrier_semaphore()

    def greet(j, carry):
        s = me ^ j
        pl.semaphore_signal(barrier, inc=1, device_id=plane_id(s), device_id_type=MESH)
        return carry

    lax.fori_loop(1, PLANE, greet, 0)
    for other in (up_id, down_id, sib_id):
        pl.semaphore_signal(barrier, inc=1, device_id=other, device_id_type=MESH)

    loads = []
    for i, (src, dst) in enumerate(
        (
            (w_hbm, w_v), (q_hbm, q_v), (kc_hbm, kc_v), (ks_hbm, ks_v), (len_hbm, len_s),
            (vc_hbm, vc_v), (vs_hbm, vs_v), (hid_hbm, hid_v),
        )
    ):
        copy = pltpu.make_async_copy(src, dst, load_sem.at[i])
        copy.start()
        loads.append(copy)
    load_w, load_q, load_kc, load_ks, load_len, load_vc, load_vs, load_hid = loads

    load_w.wait()
    for t in range(TENSORS):
        stage[t] = w_v[:, t * QB:(t + 1) * QB]
    load_q.wait()
    pl.semaphore_wait(barrier, PLANE - 1 + 3)

    def pair_copy(i, src, dst):
        return pltpu.make_async_remote_copy(
            src_ref=src, dst_ref=dst, send_sem=pair_send.at[i], recv_sem=pair_recv.at[i],
            device_id=pair_id, device_id_type=MESH,
        )

    query_copy = pair_copy(0, q_v, pq_v)
    query_copy.start()

    def block_copy(j):
        s = me ^ j
        return pltpu.make_async_remote_copy(
            src_ref=stage.at[s % TENSORS], dst_ref=landed.at[me],
            send_sem=a_send.at[j], recv_sem=a_recv.at[j],
            device_id=plane_id(s), device_id_type=MESH,
        )

    def send_block(i, carry):
        block_copy(PLANE - 1 - i).start()
        return carry

    lax.fori_loop(0, PLANE - 1, send_block, 0)
    landed[me] = stage[ten]

    root = math.sqrt(QB)
    load_len.wait()
    load_kc.wait()
    load_ks.wait()
    for h in range(HEADS):
        qs[pl.ds(h, 16, stride=8), :] = q_v[:, h * QB:(h + 1) * QB].astype(jnp.float32)
    query_copy.wait_recv()
    for h in range(HEADS):
        qs[pl.ds(HEADS + h, 16, stride=8), :] = pq_v[:, h * QB:(h + 1) * QB].astype(jnp.float32)
    position = lax.broadcasted_iota(jnp.int32, (8, QB), 1) + half * QB
    lane = lax.broadcasted_iota(jnp.int32, (8, QB), 1)
    load_vc.wait()
    load_vs.wait()
    for r in range(16):
        q_r = qs[pl.ds(r * 8, 8), :].astype(jnp.bfloat16)
        k_r = kc_v[r, 0].astype(jnp.float32).astype(jnp.bfloat16)
        score = lax.dot_general(
            q_r, k_r, (((1,), (1,)), ((), ())), preferred_element_type=jnp.float32
        )
        score = score * (ks_v[r] * (1.0 / root))
        live = position < len_s[r]
        score = jnp.where(live, score, MASKED)
        peak = jnp.max(score, axis=1, keepdims=True)
        weight = jnp.where(live, jnp.exp(score - peak), 0.0)
        total = jnp.sum(weight, axis=1, keepdims=True)
        weight = weight * vs_v[r]
        high = weight.astype(jnp.bfloat16).astype(jnp.float32)
        both = jnp.concatenate([high, weight - high], axis=0).astype(jnp.bfloat16)
        v_r = vc_v[r, 0].astype(jnp.float32).astype(jnp.bfloat16)
        out = jnp.dot(both, v_r, preferred_element_type=jnp.float32)
        osc[pl.ds(r * 8, 8), :] = out[:8] + out[8:]
        mlsc[pl.ds(r * 8, 8), :] = jnp.where(lane < 64, peak, total)

    lane16 = lax.broadcasted_iota(jnp.int32, (16, QB), 1)
    small = jnp.zeros((16, QB), jnp.float32)
    for h in range(HEADS):
        psend[h] = osc[pl.ds(HEADS + h, 16, stride=8), :]
        ml = mlsc[pl.ds(HEADS + h, 16, stride=8), :]
        here = lane16 // 32 == h
        first = (lane16 // 16) % 2 == 0
        small = jnp.where(here, jnp.where(first, ml[:, 0:1], ml[:, 64:65]), small)
    psend[HEADS] = small
    partial_copy = pair_copy(1, psend, precv)
    partial_copy.start()

    row16 = lax.broadcasted_iota(jnp.int32, (16, QB), 0)
    length = jnp.zeros((16, QB), jnp.float32)
    for r in range(16):
        length = jnp.where(row16 == r, len_s[r].astype(jnp.float32), length)
    freq_index = (lane16 % 64).astype(jnp.float32)
    angle = length * jnp.exp(freq_index * (-math.log(ROPE_BASE) / 64.0))
    cosine = jnp.cos(angle)
    sine = jnp.where(lane16 < 64, -jnp.sin(angle), jnp.sin(angle))

    def rows_of(yy, zz, cc):
        return gathered.at[pl.ds(pl.multiple_of(replica_of(yy, zz, cc) * 160, 160), 160), :]

    def ring_copy(d, k, z):
        origin = (y + NY - k) % NY if d == 0 else (y + k) % NY
        ref = rows_of(origin, z, core)
        return pltpu.make_async_remote_copy(
            src_ref=ref, dst_ref=ref,
            send_sem=ring_send.at[d, k, z], recv_sem=ring_recv.at[d, k, z],
            device_id=up_id if d == 0 else down_id, device_id_type=MESH,
        )

    def sib_copy(i, origin, z):
        ref = rows_of(origin, z, core)
        return pltpu.make_async_remote_copy(
            src_ref=ref, dst_ref=ref, send_sem=sib_send.at[i, z], recv_sem=sib_recv.at[i, z],
            device_id=sib_id, device_id_type=MESH,
        )

    sends = []

    def launch(copy):
        copy.start()
        sends.append(copy)

    def wait_block(j, carry):
        block_copy(j).wait_recv()
        return carry

    lax.fori_loop(1, PLANE, wait_block, 0)
    for z in range(2):
        for t in range(TENSORS):
            packed[pl.ds((z * TENSORS + t) * 10, 10), :] = landed[z * TENSORS + t].astype(jnp.float32)
        gathered[pl.ds(pl.multiple_of(replica_of(y, z, core) * 160, 160), 160), :] = packed[
            pl.ds(z * 160, 160), :
        ].astype(jnp.bfloat16)
        launch(ring_copy(0, 0, z))
        launch(ring_copy(1, 0, z))
        launch(sib_copy(0, y, z))

    load_hid.wait()

    def process(i, origin, projected):
        for z in range(2):
            sib_copy(i, origin, z).wait_recv()
        base = pl.multiple_of(origin * 640, 640)
        for b in range(5):
            x = gathered[pl.ds(pl.multiple_of(base + b * QB, QB), QB), :].astype(jnp.float32)
            scale = jnp.max(jnp.abs(x), axis=(0, 1), keepdims=True) + EPSILON
            q = (x * (1.0 / scale)).astype(jnp.bfloat16)
            synced_out[pl.ds(pl.multiple_of(base + b * QB, QB), QB), :] = q
            h = hid_v[:, pl.ds(pl.multiple_of(base + b * QB, QB), QB)]
            part = jnp.dot(h, q, preferred_element_type=jnp.float32)
            projected = projected + part * scale
            scale_v[pl.ds(origin * 5 + b, 1), :] = jnp.broadcast_to(scale, (1, QB))
        return projected

    def forward(d, k, z):
        ring_copy(d, k, z).wait_recv()
        origin = (y + NY - k - 1) % NY if d == 0 else (y + k + 1) % NY
        if k < 2 or (k == 2 and z == d):
            launch(ring_copy(d, k + 1, z))
        launch(sib_copy(origin_index(d, k), origin, z))

    def origin_index(d, k):
        return 7 if k == 3 else 1 + 2 * k + d

    projected = jnp.zeros((16, QB), jnp.float32)
    order = (0, 1)
    waiting = [(0, y)]
    for k in range(3):
        for z in range(2):
            for d in order:
                forward(d, k, z if d == 0 else 1 - z)
            if waiting:
                projected = process(*waiting.pop(0), projected)
        waiting += [(origin_index(0, k), (y + NY - k - 1) % NY), (origin_index(1, k), (y + k + 1) % NY)]
    for d in order:
        forward(d, 3, d)
    waiting.append((7, (y + 4) % NY))

    for item in waiting[:-1]:
        projected = process(*item, projected)
    partial_copy.wait_recv()
    merged = []
    for h in range(HEADS):
        own = osc[pl.ds(h, 16, stride=8), :]
        ml = mlsc[pl.ds(h, 16, stride=8), :]
        own_peak, own_total = ml[:, 0:1], ml[:, 64:65]
        peer_peak = precv[HEADS, :, 32 * h:32 * h + 1]
        peer_total = precv[HEADS, :, 32 * h + 16:32 * h + 17]
        joint = jnp.maximum(own_peak, peer_peak)
        own_factor = jnp.exp(own_peak - joint)
        peer_factor = jnp.exp(peer_peak - joint)
        merged.append(
            (
                joint,
                own_total * own_factor + peer_total * peer_factor,
                own * own_factor + precv[h] * peer_factor,
            )
        )
    projected = process(*waiting[-1], projected)

    rotated = projected * cosine + pltpu.roll(projected, 64, 1) * sine
    esend[...] = jnp.where(half == 1, projected, rotated).astype(jnp.bfloat16)
    entry_copy = pair_copy(2, esend, erecv)
    entry_copy.start()
    scale_out[...] = scale_v[:, 0:1]
    for copy in sends:
        copy.wait_send()
    query_copy.wait_send()
    partial_copy.wait_send()

    def drain(j, carry):
        block_copy(j).wait_send()
        return carry

    lax.fori_loop(1, PLANE, drain, 0)
    entry_copy.wait()
    own = esend[...].astype(jnp.float32)
    other = erecv[...].astype(jnp.float32)
    key = jnp.where(half == 1, other, own)
    value = jnp.where(half == 1, own, other)
    for h in range(HEADS):
        joint, total, weighted = merged[h]
        q_h = q_v[:, h * QB:(h + 1) * QB].astype(jnp.float32)
        score = jnp.sum(q_h * key, axis=1, keepdims=True) / root
        peak = jnp.maximum(joint, score)
        cached = jnp.exp(joint - peak)
        fresh = jnp.exp(score - peak)
        result = (weighted * cached + fresh * value) / (total * cached + fresh)
        att_out[:, h * QB:(h + 1) * QB] = result.astype(jnp.bfloat16)


def shards(*args):
    rows, depth = args[1].shape
    bf16, f32 = jnp.bfloat16, jnp.float32
    hbm = pl.BlockSpec(memory_space=pltpu.HBM)
    vmem = pl.BlockSpec(memory_space=pltpu.VMEM)
    dma = pltpu.SemaphoreType.DMA
    return pl.pallas_call(
        kernel,
        out_shape=(
            jax.ShapeDtypeStruct((depth, QB), bf16),
            jax.ShapeDtypeStruct((depth // QB, 1), f32),
            jax.ShapeDtypeStruct((rows, HEADS * QB), bf16),
        ),
        in_specs=[hbm] * 8,
        out_specs=(vmem, vmem, vmem),
        scratch_shapes=[
            pltpu.VMEM((10, 2048), bf16),
            pltpu.VMEM((rows, depth), bf16),
            pltpu.VMEM((rows, HEADS * QB), bf16),
            pltpu.VMEM((rows, HEADS * QB), bf16),
            pltpu.VMEM((rows, 1, QB, QB), jnp.int32),
            pltpu.VMEM((rows, 1, QB), f32),
            pltpu.VMEM((rows, 1, QB, QB), jnp.int32),
            pltpu.VMEM((rows, 1, QB), f32),
            pltpu.SMEM((rows,), jnp.int32),
            pltpu.VMEM((TENSORS, 10, QB), bf16),
            pltpu.VMEM((PLANE, 10, QB), bf16),
            pltpu.VMEM((320, QB), f32),
            pltpu.VMEM((depth, QB), bf16),
            pltpu.VMEM((depth // QB, QB), f32),
            pltpu.VMEM((128, QB), f32),
            pltpu.VMEM((128, QB), f32),
            pltpu.VMEM((128, QB), f32),
            pltpu.VMEM((HEADS + 1, rows, QB), f32),
            pltpu.VMEM((HEADS + 1, rows, QB), f32),
            pltpu.VMEM((rows, QB), bf16),
            pltpu.VMEM((rows, QB), bf16),
            dma((8,)),
            dma((PLANE,)),
            dma((PLANE,)),
            dma((2, 4, 2)),
            dma((2, 4, 2)),
            dma((8, 2)),
            dma((8, 2)),
            dma((3,)),
            dma((3,)),
        ],
        compiler_params=pltpu.CompilerParams(
            collective_id=0, has_side_effects=True, vmem_limit_bytes=62000000
        ),
        cost_estimate=pl.CostEstimate(flops=60000000, bytes_accessed=6000000, transcendentals=100000),
        name="sync_decode",
    )(*args)


def solution(mesh):
    placed = (
        P(("replica", "tensor"), None),
        P("replica", None),
        P("replica", "tensor"),
        P("replica", "tensor", None, None),
        P("replica", "tensor", None),
        P("replica", "tensor", None, None),
        P("replica", "tensor", None),
        P("replica"),
    )
    return jax.shard_map(
        shards,
        mesh=mesh,
        in_specs=placed,
        out_specs=(P(None, "tensor"), P(None, "tensor"), P("replica", "tensor")),
        check_vma=False,
    )
```

```python
import math

import jax
import jax.numpy as jnp
from jax import lax
from jax.experimental import pallas as pl
from jax.experimental.pallas import tpu as pltpu
from jax.sharding import PartitionSpec as P

HEADS = 4
QB = 128
EPSILON = 1e-06
ROPE_BASE = 1000000.0
MASKED = -1e30
MESH = pl.DeviceIdType.MESH

NY = 8
NX = 4
NZ = 8
ZLO = 4
TENSORS = 16
SEND_ORDER = (2, 6, 1, 7, 0, 3, 5, 4)
LAST = 7


def kernel(
    w_hbm, hid_hbm, q_hbm, kc_hbm, ks_hbm, vc_hbm, vs_hbm, len_hbm,
    synced_out, scale_out, att_out,
    w_v, hid_v, q_v, pq_v, kc_v, ks_v, vc_v, vs_v, len_s,
    stage, landed, packed, gathered, group, scale_v,
    qs, osc, mlsc, psend, precv, esend, erecv,
    load_sem, plane_send, plane_recv, ring_send, ring_recv, sib_send, sib_recv,
    pair_send, pair_recv,
):
    rep = lax.axis_index("replica")
    ten = lax.axis_index("tensor")
    y = rep // 4
    zhi = (rep // 2) % 2
    core = rep % 2
    half = ten % 2
    x = ten % NX
    z = zhi * ZLO + ten // NX

    def replica_of(yy, zz, cc):
        return (yy * 2 + zz) * 2 + cc

    def plane_id(zz, xx):
        return {"replica": replica_of(y, zz // ZLO, core), "tensor": (zz % ZLO) * NX + xx}

    def along_y(steps):
        return {"replica": replica_of((y + NY + steps) % NY, zhi, core), "tensor": ten}

    sib_id = {"replica": replica_of(y, zhi, 1 - core), "tensor": ten}
    pair_id = plane_id(z, x ^ 1)

    loads = [
        pltpu.make_async_copy(src, dst, load_sem.at[i])
        for i, (src, dst) in enumerate(
            (
                (w_hbm, w_v), (q_hbm, q_v), (kc_hbm, kc_v), (ks_hbm, ks_v), (len_hbm, len_s),
                (vc_hbm, vc_v), (vs_hbm, vs_v), (hid_hbm, hid_v),
            )
        )
    ]
    load_w, load_q, load_kc, load_ks, load_len, load_vc, load_vs, load_hid = loads
    load_w.start()
    load_q.start()

    barrier = pltpu.get_barrier_semaphore()
    peers = [
        plane_id((z + dz) % NZ, x ^ dx)
        for dz in (4, 3, 5, 2, 6, 1, 7, 0) for dx in (2, 3, 1, 0) if dz or dx
    ]
    peers += [along_y(2), along_y(-2), along_y(1), along_y(-1), sib_id]
    for other in peers:
        pl.semaphore_signal(barrier, inc=1, device_id=other, device_id_type=MESH)
    for copy in loads[2:]:
        copy.start()

    load_w.wait()
    for t in range(TENSORS):
        stage[t] = w_v[:, t * QB:(t + 1) * QB]
    load_q.wait()
    pl.semaphore_wait(barrier, len(peers))

    sends = []

    def launch(copy):
        copy.start()
        sends.append(copy)

    def pair_copy(i, src, dst):
        return pltpu.make_async_remote_copy(
            src_ref=src, dst_ref=dst, send_sem=pair_send.at[i], recv_sem=pair_recv.at[i],
            device_id=pair_id, device_id_type=MESH,
        )

    def plane_copy(j):
        to_z, to_x = (z + j // NX) % NZ, x ^ (j % NX)
        return pltpu.make_async_remote_copy(
            src_ref=stage.at[(to_z % ZLO) * NX + to_x], dst_ref=landed.at[z * NX + x],
            send_sem=plane_send.at[j], recv_sem=plane_recv.at[j],
            device_id=plane_id(to_z, to_x), device_id_type=MESH,
        )

    query_copy = pair_copy(0, q_v, pq_v)
    launch(query_copy)
    for dz in SEND_ORDER:
        for dx in (2, 3, 1, 0):
            if dz or dx:
                launch(plane_copy(dz * NX + dx))
    landed[z * NX + x] = stage[ten]

    root = math.sqrt(QB)
    load_len.wait()
    load_kc.wait()
    load_ks.wait()
    for h in range(HEADS):
        qs[pl.ds(h, 16, stride=8), :] = q_v[:, h * QB:(h + 1) * QB].astype(jnp.float32)
    query_copy.wait_recv()
    for h in range(HEADS):
        qs[pl.ds(HEADS + h, 16, stride=8), :] = pq_v[:, h * QB:(h + 1) * QB].astype(jnp.float32)
    position = lax.broadcasted_iota(jnp.int32, (8, QB), 1) + half * QB
    lane = lax.broadcasted_iota(jnp.int32, (8, QB), 1)
    load_vc.wait()
    load_vs.wait()
    for r in range(16):
        q_r = qs[pl.ds(r * 8, 8), :].astype(jnp.bfloat16)
        k_r = kc_v[r, 0].astype(jnp.float32).astype(jnp.bfloat16)
        score = lax.dot_general(
            q_r, k_r, (((1,), (1,)), ((), ())), preferred_element_type=jnp.float32
        )
        score = score * (ks_v[r] * (1.0 / root))
        live = position < len_s[r]
        score = jnp.where(live, score, MASKED)
        peak = jnp.max(score, axis=1, keepdims=True)
        weight = jnp.where(live, jnp.exp(score - peak), 0.0)
        total = jnp.sum(weight, axis=1, keepdims=True)
        weight = weight * vs_v[r]
        high = weight.astype(jnp.bfloat16).astype(jnp.float32)
        both = jnp.concatenate([high, weight - high], axis=0).astype(jnp.bfloat16)
        v_r = vc_v[r, 0].astype(jnp.float32).astype(jnp.bfloat16)
        out = jnp.dot(both, v_r, preferred_element_type=jnp.float32)
        osc[pl.ds(r * 8, 8), :] = out[:8] + out[8:]
        mlsc[pl.ds(r * 8, 8), :] = jnp.where(lane < 64, peak, total)

    lane16 = lax.broadcasted_iota(jnp.int32, (16, QB), 1)
    small = jnp.zeros((16, QB), jnp.float32)
    for h in range(HEADS):
        psend[h] = osc[pl.ds(HEADS + h, 16, stride=8), :]
        ml = mlsc[pl.ds(HEADS + h, 16, stride=8), :]
        here = lane16 // 32 == h
        first = (lane16 // 16) % 2 == 0
        small = jnp.where(here, jnp.where(first, ml[:, 0:1], ml[:, 64:65]), small)
    psend[HEADS] = small
    partial_copy = pair_copy(1, psend, precv)
    launch(partial_copy)

    near = z // 2
    odd = z % 2
    pairs = (near, (near + 3 + 2 * odd) % 4, (near + 1 + 2 * odd) % 4, (near + 2) % 4)

    def chunk(yy, cc, piece):
        base = (yy * 2 + cc) * 320 + (160 if piece == 1 else 0)
        return pl.ds(pl.multiple_of(base, 160), 320 if piece is None else 160)

    def origin_of(d, k):
        return (y + NY - k) % NY if d == 0 else (y + k) % NY

    def ring_copy(piece, d, k):
        leg = 2 if k % 2 == 0 else 1
        ref = gathered.at[chunk(origin_of(d, k - leg), core, piece), :]
        return pltpu.make_async_remote_copy(
            src_ref=ref, dst_ref=ref,
            send_sem=ring_send.at[d, k - 1, piece], recv_sem=ring_recv.at[d, k - 1, piece],
            device_id=along_y(leg if d == 0 else -leg), device_id_type=MESH,
        )

    def arrived(piece, d, k):
        leg = 2 if k % 2 == 0 else 1
        ref = gathered.at[chunk(origin_of(d, k), core, piece), :]
        pltpu.make_async_remote_copy(
            src_ref=ref, dst_ref=ref,
            send_sem=ring_send.at[d, k - 1, piece], recv_sem=ring_recv.at[d, k - 1, piece],
            device_id=along_y(leg if d == 0 else -leg), device_id_type=MESH,
        ).wait_recv()

    def sib_copy(i, origin, piece, cc):
        ref = gathered.at[chunk(origin, cc, piece), :]
        return pltpu.make_async_remote_copy(
            src_ref=ref, dst_ref=ref, send_sem=sib_send.at[i], recv_sem=sib_recv.at[i],
            device_id=sib_id, device_id_type=MESH,
        )

    def plane_wait(dz):
        for dx in range(NX):
            plane_copy(dz * NX + dx).wait_recv()

    def start_piece(piece):
        for i in range(2):
            for side in range(2):
                for e in range(NX):
                    packed[pl.ds((2 * i + side) * 40 + e * 10, 10), :] = landed[
                        (2 * pairs[2 * piece + i] + side) * NX + e
                    ].astype(jnp.float32)
        gathered[chunk(y, core, piece), :] = packed[...].astype(jnp.bfloat16)
        for k in (2, 1):
            for d in range(2):
                launch(ring_copy(piece, d, k))

    for dx in range(1, NX):
        plane_copy(dx).wait_recv()
    for dz in (1, 7, 2 + 4 * odd):
        plane_wait(dz)
    start_piece(0)
    for dz in (6 - 4 * odd, 3, 5, 4):
        plane_wait(dz)
    start_piece(1)
    launch(sib_copy(0, y, None, core))

    row16 = lax.broadcasted_iota(jnp.int32, (16, QB), 0)
    length = jnp.zeros((16, QB), jnp.float32)
    for r in range(16):
        length = jnp.where(row16 == r, len_s[r].astype(jnp.float32), length)
    freq_index = (lane16 % 64).astype(jnp.float32)
    angle = length * jnp.exp(freq_index * (-math.log(ROPE_BASE) / 64.0))
    cosine = jnp.cos(angle)
    sine = jnp.where(lane16 < 64, -jnp.sin(angle), jnp.sin(angle))

    load_hid.wait()

    def process(i, origin, projected):
        if i == LAST:
            for piece in range(2):
                sib_copy(LAST + piece, origin, piece, 1 - core).wait_recv()
        else:
            sib_copy(i, origin, None, 1 - core).wait_recv()
        for cc in range(2):
            for q in range(4):
                to = (pairs[q] // 2) * 320 + cc * 160 + (pairs[q] % 2) * 80
                at = (origin * 2 + cc) * 320 + q * 80
                group[pl.ds(pl.multiple_of(to, 80), 80), :] = gathered[pl.ds(pl.multiple_of(at, 80), 80), :]
        base = pl.multiple_of(origin * 640, 640)
        for b in range(5):
            raw = group[pl.ds(b * QB, QB), :].astype(jnp.float32)
            scale = jnp.max(jnp.abs(raw), axis=(0, 1), keepdims=True) + EPSILON
            q = (raw * (1.0 / scale)).astype(jnp.bfloat16)
            synced_out[pl.ds(pl.multiple_of(base + b * QB, QB), QB), :] = q
            h = hid_v[:, pl.ds(pl.multiple_of(base + b * QB, QB), QB)]
            part = jnp.dot(h, q, preferred_element_type=jnp.float32)
            projected = projected + part * scale
            scale_v[pl.ds(origin * 5 + b, 1), :] = jnp.broadcast_to(scale, (1, QB))
        return projected

    def receive(piece, k):
        for d in (0, 1) if k < 4 else (1 - piece,):
            arrived(piece, d, k)
            if k == 2:
                if d == 1 - piece:
                    launch(ring_copy(piece, d, 4))
                launch(ring_copy(piece, d, 3))
        if k == 4:
            launch(sib_copy(LAST + piece, origin_of(0, 4), piece, core))

    def share(k):
        for d in range(2):
            launch(sib_copy(2 * k - 1 + d, origin_of(d, k), None, core))

    projected = jnp.zeros((16, QB), jnp.float32)
    receive(0, 2)
    receive(0, 1)
    receive(1, 2)
    share(2)
    receive(1, 1)
    share(1)
    projected = process(0, y, projected)
    receive(0, 3)
    for d in range(2):
        projected = process(3 + d, origin_of(d, 2), projected)
    receive(1, 3)
    share(3)
    for d in range(2):
        projected = process(1 + d, origin_of(d, 1), projected)
    receive(0, 4)
    receive(1, 4)
    for d in range(2):
        projected = process(5 + d, origin_of(d, 3), projected)

    partial_copy.wait_recv()
    merged = []
    for h in range(HEADS):
        own = osc[pl.ds(h, 16, stride=8), :]
        ml = mlsc[pl.ds(h, 16, stride=8), :]
        own_peak, own_total = ml[:, 0:1], ml[:, 64:65]
        peer_peak = precv[HEADS, :, 32 * h:32 * h + 1]
        peer_total = precv[HEADS, :, 32 * h + 16:32 * h + 17]
        joint = jnp.maximum(own_peak, peer_peak)
        own_factor = jnp.exp(own_peak - joint)
        peer_factor = jnp.exp(peer_peak - joint)
        merged.append(
            (
                joint,
                own_total * own_factor + peer_total * peer_factor,
                own * own_factor + precv[h] * peer_factor,
            )
        )
    projected = process(LAST, origin_of(0, 4), projected)

    rotated = projected * cosine + pltpu.roll(projected, 64, 1) * sine
    esend[...] = jnp.where(half == 1, projected, rotated).astype(jnp.bfloat16)
    entry_copy = pair_copy(2, esend, erecv)
    entry_copy.start()
    scale_out[...] = jnp.transpose(scale_v[...], (1, 0))[0:1, 0:40]
    for copy in sends:
        copy.wait_send()
    entry_copy.wait()
    own = esend[...].astype(jnp.float32)
    other = erecv[...].astype(jnp.float32)
    key = jnp.where(half == 1, other, own)
    value = jnp.where(half == 1, own, other)
    for h in range(HEADS):
        joint, total, weighted = merged[h]
        q_h = q_v[:, h * QB:(h + 1) * QB].astype(jnp.float32)
        score = jnp.sum(q_h * key, axis=1, keepdims=True) / root
        peak = jnp.maximum(joint, score)
        cached = jnp.exp(joint - peak)
        fresh = jnp.exp(score - peak)
        result = (weighted * cached + fresh * value) / (total * cached + fresh)
        att_out[:, h * QB:(h + 1) * QB] = result.astype(jnp.bfloat16)


PARTS = 4


def settle(synced, scales, attended, synced_out, scales_out, attended_out, sem):
    step = synced.shape[0] // PARTS
    legs = [(scales, scales_out), (attended, attended_out)]
    legs += [(ref.at[pl.ds(i * step, step), :], out.at[pl.ds(i * step, step), :])
             for ref, out in ((synced, synced_out),) for i in range(PARTS)]
    copies = [pltpu.make_async_copy(one, other, sem.at[i]) for i, (one, other) in enumerate(legs)]
    for copy in copies:
        copy.start()
    for copy in copies:
        copy.wait()


def shards(*args):
    rows, depth = args[1].shape
    bf16, f32 = jnp.bfloat16, jnp.float32
    hbm = pl.BlockSpec(memory_space=pltpu.HBM)
    vmem = pl.BlockSpec(memory_space=pltpu.VMEM)
    dma = pltpu.SemaphoreType.DMA
    synced, scales, attended = pl.pallas_call(
        kernel,
        out_shape=(
            pltpu.VMEM((depth, QB), bf16),
            pltpu.VMEM((1, depth // QB), f32),
            pltpu.VMEM((rows, HEADS * QB), bf16),
        ),
        in_specs=[hbm] * 8,
        out_specs=(vmem, vmem, vmem),
        scratch_shapes=[
            pltpu.VMEM((10, 2048), bf16),
            pltpu.VMEM((rows, depth), bf16),
            pltpu.VMEM((rows, HEADS * QB), bf16),
            pltpu.VMEM((rows, HEADS * QB), bf16),
            pltpu.VMEM((rows, 1, QB, QB), jnp.int32),
            pltpu.VMEM((rows, 1, QB), f32),
            pltpu.VMEM((rows, 1, QB, QB), jnp.int32),
            pltpu.VMEM((rows, 1, QB), f32),
            pltpu.SMEM((rows,), jnp.int32),
            pltpu.VMEM((TENSORS, 10, QB), bf16),
            pltpu.VMEM((NZ * NX, 10, QB), bf16),
            pltpu.VMEM((160, QB), f32),
            pltpu.VMEM((depth, QB), bf16),
            pltpu.VMEM((640, QB), bf16),
            pltpu.VMEM((128, QB), f32),
            pltpu.VMEM((128, QB), f32),
            pltpu.VMEM((128, QB), f32),
            pltpu.VMEM((128, QB), f32),
            pltpu.VMEM((HEADS + 1, rows, QB), f32),
            pltpu.VMEM((HEADS + 1, rows, QB), f32),
            pltpu.VMEM((rows, QB), bf16),
            pltpu.VMEM((rows, QB), bf16),
            dma((8,)),
            dma((NZ * NX,)),
            dma((NZ * NX,)),
            dma((2, 4, 2)),
            dma((2, 4, 2)),
            dma((9,)),
            dma((9,)),
            dma((3,)),
            dma((3,)),
        ],
        compiler_params=pltpu.CompilerParams(
            collective_id=0, has_side_effects=True, vmem_limit_bytes=62000000
        ),
        cost_estimate=pl.CostEstimate(flops=60000000, bytes_accessed=6000000, transcendentals=100000),
        name="sync_decode",
    )(*args)
    synced, scales, attended = pl.pallas_call(
        settle,
        out_shape=(
            jax.ShapeDtypeStruct((depth, QB), bf16),
            jax.ShapeDtypeStruct((1, depth // QB), f32),
            jax.ShapeDtypeStruct((rows, HEADS * QB), bf16),
        ),
        in_specs=[vmem] * 3,
        out_specs=(hbm,) * 3,
        scratch_shapes=[dma((PARTS + 2,))],
        compiler_params=pltpu.CompilerParams(vmem_limit_bytes=8 * 1024 * 1024),
        name="settle",
    )(synced, scales, attended)
    return synced, scales.reshape(depth // QB, 1), attended


def solution(mesh):
    placed = (
        P(("replica", "tensor"), None),
        P("replica", None),
        P("replica", "tensor"),
        P("replica", "tensor", None, None),
        P("replica", "tensor", None),
        P("replica", "tensor", None, None),
        P("replica", "tensor", None),
        P("replica"),
    )
    return jax.shard_map(
        shards,
        mesh=mesh,
        in_specs=placed,
        out_specs=(P(None, "tensor"), P(None, "tensor"), P("replica", "tensor")),
        check_vma=False,
    )
```

```python
import math

import jax
import jax.numpy as jnp
from jax import lax
from jax.experimental import pallas as pl
from jax.experimental.pallas import tpu as pltpu
from jax.sharding import PartitionSpec as P

HEADS = 4
QB = 128
EPSILON = 1e-06
ROPE_BASE = 1000000.0
MASKED = -1e30
MESH = pl.DeviceIdType.MESH

NY = 8
NX = 4
NZ = 8
ZLO = 4
TENSORS = 16
SEND_ORDER = (2, 6, 1, 7, 0, 3, 5, 4)
LAST = 7


def kernel(
    w_hbm, hid_hbm, q_hbm, kc_hbm, ks_hbm, vc_hbm, vs_hbm, len_hbm,
    synced_out, scale_out, att_out,
    w_v, hid_v, q_v, pq_v, kc_v, ks_v, vc_v, vs_v, len_s,
    stage, landed, packed, gathered, group, scale_v,
    qs, osc, mlsc, psend, precv, esend, erecv,
    load_sem, plane_send, plane_recv, ring_send, ring_recv, sib_send, sib_recv,
    pair_send, pair_recv,
):
    rep = lax.axis_index("replica")
    ten = lax.axis_index("tensor")
    y = rep // 4
    zhi = (rep // 2) % 2
    core = rep % 2
    half = ten % 2
    x = ten % NX
    z = zhi * ZLO + ten // NX

    def replica_of(yy, zz, cc):
        return (yy * 2 + zz) * 2 + cc

    def plane_id(zz, xx):
        return {"replica": replica_of(y, zz // ZLO, core), "tensor": (zz % ZLO) * NX + xx}

    def along_y(steps):
        return {"replica": replica_of((y + NY + steps) % NY, zhi, core), "tensor": ten}

    sib_id = {"replica": replica_of(y, zhi, 1 - core), "tensor": ten}
    pair_id = plane_id(z, x ^ 1)

    loads = [
        pltpu.make_async_copy(src, dst, load_sem.at[i])
        for i, (src, dst) in enumerate(
            (
                (w_hbm, w_v), (q_hbm, q_v), (kc_hbm, kc_v), (ks_hbm, ks_v), (len_hbm, len_s),
                (vc_hbm, vc_v), (vs_hbm, vs_v), (hid_hbm, hid_v),
            )
        )
    ]
    load_w, load_q, load_kc, load_ks, load_len, load_vc, load_vs, load_hid = loads
    load_w.start()
    load_q.start()

    barrier = pltpu.get_barrier_semaphore()
    peers = [
        plane_id((z + dz) % NZ, x ^ dx)
        for dz in (4, 3, 5, 2, 6, 1, 7, 0) for dx in (2, 3, 1, 0) if dz or dx
    ]
    peers += [along_y(2), along_y(-2), along_y(1), along_y(-1), sib_id]
    for other in peers:
        pl.semaphore_signal(barrier, inc=1, device_id=other, device_id_type=MESH)
    for copy in loads[2:]:
        copy.start()

    load_w.wait()
    for t in range(TENSORS):
        stage[t] = w_v[:, t * QB:(t + 1) * QB]
    load_q.wait()
    pl.semaphore_wait(barrier, len(peers))

    sends = []

    def launch(copy):
        copy.start()
        sends.append(copy)

    def pair_copy(i, src, dst):
        return pltpu.make_async_remote_copy(
            src_ref=src, dst_ref=dst, send_sem=pair_send.at[i], recv_sem=pair_recv.at[i],
            device_id=pair_id, device_id_type=MESH,
        )

    def plane_copy(j):
        to_z, to_x = (z + j // NX) % NZ, x ^ (j % NX)
        return pltpu.make_async_remote_copy(
            src_ref=stage.at[(to_z % ZLO) * NX + to_x], dst_ref=landed.at[z * NX + x],
            send_sem=plane_send.at[j], recv_sem=plane_recv.at[j],
            device_id=plane_id(to_z, to_x), device_id_type=MESH,
        )

    query_copy = pair_copy(0, q_v, pq_v)
    launch(query_copy)
    for dz in SEND_ORDER:
        for dx in (2, 3, 1, 0):
            if dz or dx:
                launch(plane_copy(dz * NX + dx))
    landed[z * NX + x] = stage[ten]

    root = math.sqrt(QB)
    position = lax.broadcasted_iota(jnp.int32, (8, QB), 1) + half * QB
    lane = lax.broadcasted_iota(jnp.int32, (8, QB), 1)
    lane16 = lax.broadcasted_iota(jnp.int32, (16, QB), 1)

    def ready_queries():
        load_len.wait()
        load_kc.wait()
        load_ks.wait()
        for h in range(HEADS):
            qs[pl.ds(h, 16, stride=8), :] = q_v[:, h * QB:(h + 1) * QB].astype(jnp.float32)
        query_copy.wait_recv()
        for h in range(HEADS):
            qs[pl.ds(HEADS + h, 16, stride=8), :] = pq_v[:, h * QB:(h + 1) * QB].astype(jnp.float32)
        load_vc.wait()
        load_vs.wait()

    def attend(first, last):
        for r in range(first, last):
            q_r = qs[pl.ds(r * 8, 8), :].astype(jnp.bfloat16)
            k_r = kc_v[r, 0].astype(jnp.float32).astype(jnp.bfloat16)
            score = lax.dot_general(
                q_r, k_r, (((1,), (1,)), ((), ())), preferred_element_type=jnp.float32
            )
            score = score * (ks_v[r] * (1.0 / root))
            live = position < len_s[r]
            score = jnp.where(live, score, MASKED)
            peak = jnp.max(score, axis=1, keepdims=True)
            weight = jnp.where(live, jnp.exp(score - peak), 0.0)
            total = jnp.sum(weight, axis=1, keepdims=True)
            weight = weight * vs_v[r]
            high = weight.astype(jnp.bfloat16).astype(jnp.float32)
            both = jnp.concatenate([high, weight - high], axis=0).astype(jnp.bfloat16)
            v_r = vc_v[r, 0].astype(jnp.float32).astype(jnp.bfloat16)
            out = jnp.dot(both, v_r, preferred_element_type=jnp.float32)
            osc[pl.ds(r * 8, 8), :] = out[:8] + out[8:]
            mlsc[pl.ds(r * 8, 8), :] = jnp.where(lane < 64, peak, total)


    partial_copy = pair_copy(1, psend, precv)

    def send_partials():
        small = jnp.zeros((16, QB), jnp.float32)
        for h in range(HEADS):
            psend[h] = osc[pl.ds(HEADS + h, 16, stride=8), :]
            ml = mlsc[pl.ds(HEADS + h, 16, stride=8), :]
            here = lane16 // 32 == h
            first = (lane16 // 16) % 2 == 0
            small = jnp.where(here, jnp.where(first, ml[:, 0:1], ml[:, 64:65]), small)
        psend[HEADS] = small
        launch(partial_copy)

    near = z // 2
    odd = z % 2
    pairs = (near, (near + 3 + 2 * odd) % 4, (near + 1 + 2 * odd) % 4, (near + 2) % 4)

    def chunk(yy, cc, piece):
        base = (yy * 2 + cc) * 320 + (160 if piece == 1 else 0)
        return pl.ds(pl.multiple_of(base, 160), 320 if piece is None else 160)

    def origin_of(d, k):
        return (y + NY - k) % NY if d == 0 else (y + k) % NY

    def ring_copy(piece, d, k):
        leg = 2 if k % 2 == 0 else 1
        ref = gathered.at[chunk(origin_of(d, k - leg), core, piece), :]
        return pltpu.make_async_remote_copy(
            src_ref=ref, dst_ref=ref,
            send_sem=ring_send.at[d, k - 1, piece], recv_sem=ring_recv.at[d, k - 1, piece],
            device_id=along_y(leg if d == 0 else -leg), device_id_type=MESH,
        )

    def arrived(piece, d, k):
        leg = 2 if k % 2 == 0 else 1
        ref = gathered.at[chunk(origin_of(d, k), core, piece), :]
        pltpu.make_async_remote_copy(
            src_ref=ref, dst_ref=ref,
            send_sem=ring_send.at[d, k - 1, piece], recv_sem=ring_recv.at[d, k - 1, piece],
            device_id=along_y(leg if d == 0 else -leg), device_id_type=MESH,
        ).wait_recv()

    def sib_copy(i, origin, piece, cc):
        ref = gathered.at[chunk(origin, cc, piece), :]
        return pltpu.make_async_remote_copy(
            src_ref=ref, dst_ref=ref, send_sem=sib_send.at[i], recv_sem=sib_recv.at[i],
            device_id=sib_id, device_id_type=MESH,
        )

    def plane_wait(dz):
        for dx in range(NX):
            plane_copy(dz * NX + dx).wait_recv()

    def start_piece(piece):
        for i in range(2):
            for side in range(2):
                for e in range(NX):
                    packed[pl.ds((2 * i + side) * 40 + e * 10, 10), :] = landed[
                        (2 * pairs[2 * piece + i] + side) * NX + e
                    ].astype(jnp.float32)
        gathered[chunk(y, core, piece), :] = packed[...].astype(jnp.bfloat16)
        for k in (2, 1):
            for d in range(2):
                launch(ring_copy(piece, d, k))

    for dx in range(1, NX):
        plane_copy(dx).wait_recv()
    for dz in (1, 7, 2 + 4 * odd):
        plane_wait(dz)
    start_piece(0)
    for dz in (6 - 4 * odd, 3, 5, 4):
        plane_wait(dz)
    start_piece(1)
    launch(sib_copy(0, y, None, core))
    ready_queries()
    attend(0, 16)
    send_partials()

    row16 = lax.broadcasted_iota(jnp.int32, (16, QB), 0)
    length = jnp.zeros((16, QB), jnp.float32)
    for r in range(16):
        length = jnp.where(row16 == r, len_s[r].astype(jnp.float32), length)
    freq_index = (lane16 % 64).astype(jnp.float32)
    angle = length * jnp.exp(freq_index * (-math.log(ROPE_BASE) / 64.0))
    cosine = jnp.cos(angle)
    sine = jnp.where(lane16 < 64, -jnp.sin(angle), jnp.sin(angle))

    load_hid.wait()

    def process(i, origin, projected):
        if i == LAST:
            for piece in range(2):
                sib_copy(LAST + piece, origin, piece, 1 - core).wait_recv()
        else:
            sib_copy(i, origin, None, 1 - core).wait_recv()
        for cc in range(2):
            for q in range(4):
                to = (pairs[q] // 2) * 320 + cc * 160 + (pairs[q] % 2) * 80
                at = (origin * 2 + cc) * 320 + q * 80
                group[pl.ds(pl.multiple_of(to, 80), 80), :] = gathered[pl.ds(pl.multiple_of(at, 80), 80), :]
        base = pl.multiple_of(origin * 640, 640)
        for b in range(5):
            raw = group[pl.ds(b * QB, QB), :].astype(jnp.float32)
            scale = jnp.max(jnp.abs(raw), axis=(0, 1), keepdims=True) + EPSILON
            q = (raw * (1.0 / scale)).astype(jnp.bfloat16)
            synced_out[pl.ds(pl.multiple_of(base + b * QB, QB), QB), :] = q
            h = hid_v[:, pl.ds(pl.multiple_of(base + b * QB, QB), QB)]
            part = jnp.dot(h, q, preferred_element_type=jnp.float32)
            projected = projected + part * scale
            scale_v[pl.ds(origin * 5 + b, 1), :] = jnp.broadcast_to(scale, (1, QB))
        return projected

    def receive(piece, k):
        for d in (0, 1) if k < 4 else (1 - piece,):
            arrived(piece, d, k)
            if k == 2:
                if d == 1 - piece:
                    launch(ring_copy(piece, d, 4))
                launch(ring_copy(piece, d, 3))
        if k == 4:
            launch(sib_copy(LAST + piece, origin_of(0, 4), piece, core))

    def share(k):
        for d in range(2):
            launch(sib_copy(2 * k - 1 + d, origin_of(d, k), None, core))

    projected = jnp.zeros((16, QB), jnp.float32)
    receive(0, 2)
    receive(0, 1)
    receive(1, 2)
    share(2)
    receive(1, 1)
    share(1)
    projected = process(0, y, projected)
    receive(0, 3)
    for d in range(2):
        projected = process(3 + d, origin_of(d, 2), projected)
    receive(1, 3)
    share(3)
    for d in range(2):
        projected = process(1 + d, origin_of(d, 1), projected)
    receive(0, 4)
    receive(1, 4)
    for d in range(2):
        projected = process(5 + d, origin_of(d, 3), projected)

    partial_copy.wait_recv()
    merged = []
    for h in range(HEADS):
        own = osc[pl.ds(h, 16, stride=8), :]
        ml = mlsc[pl.ds(h, 16, stride=8), :]
        own_peak, own_total = ml[:, 0:1], ml[:, 64:65]
        peer_peak = precv[HEADS, :, 32 * h:32 * h + 1]
        peer_total = precv[HEADS, :, 32 * h + 16:32 * h + 17]
        joint = jnp.maximum(own_peak, peer_peak)
        own_factor = jnp.exp(own_peak - joint)
        peer_factor = jnp.exp(peer_peak - joint)
        merged.append(
            (
                joint,
                own_total * own_factor + peer_total * peer_factor,
                own * own_factor + precv[h] * peer_factor,
            )
        )
    projected = process(LAST, origin_of(0, 4), projected)

    rotated = projected * cosine + pltpu.roll(projected, 64, 1) * sine
    esend[...] = jnp.where(half == 1, projected, rotated).astype(jnp.bfloat16)
    entry_copy = pair_copy(2, esend, erecv)
    entry_copy.start()
    scale_out[...] = jnp.transpose(scale_v[...], (1, 0))[0:1, 0:40]
    for copy in sends:
        copy.wait_send()
    entry_copy.wait()
    own = esend[...].astype(jnp.float32)
    other = erecv[...].astype(jnp.float32)
    key = jnp.where(half == 1, other, own)
    value = jnp.where(half == 1, own, other)
    for h in range(HEADS):
        joint, total, weighted = merged[h]
        q_h = q_v[:, h * QB:(h + 1) * QB].astype(jnp.float32)
        score = jnp.sum(q_h * key, axis=1, keepdims=True) / root
        peak = jnp.maximum(joint, score)
        cached = jnp.exp(joint - peak)
        fresh = jnp.exp(score - peak)
        result = (weighted * cached + fresh * value) / (total * cached + fresh)
        att_out[:, h * QB:(h + 1) * QB] = result.astype(jnp.bfloat16)


PARTS = 4


def settle(synced, scales, attended, synced_out, scales_out, attended_out, sem):
    step = synced.shape[0] // PARTS
    legs = [(scales, scales_out), (attended, attended_out)]
    legs += [(ref.at[pl.ds(i * step, step), :], out.at[pl.ds(i * step, step), :])
             for ref, out in ((synced, synced_out),) for i in range(PARTS)]
    copies = [pltpu.make_async_copy(one, other, sem.at[i]) for i, (one, other) in enumerate(legs)]
    for copy in copies:
        copy.start()
    for copy in copies:
        copy.wait()


def shards(*args):
    rows, depth = args[1].shape
    bf16, f32 = jnp.bfloat16, jnp.float32
    hbm = pl.BlockSpec(memory_space=pltpu.HBM)
    vmem = pl.BlockSpec(memory_space=pltpu.VMEM)
    dma = pltpu.SemaphoreType.DMA
    synced, scales, attended = pl.pallas_call(
        kernel,
        out_shape=(
            pltpu.VMEM((depth, QB), bf16),
            pltpu.VMEM((1, depth // QB), f32),
            pltpu.VMEM((rows, HEADS * QB), bf16),
        ),
        in_specs=[hbm] * 8,
        out_specs=(vmem, vmem, vmem),
        scratch_shapes=[
            pltpu.VMEM((10, 2048), bf16),
            pltpu.VMEM((rows, depth), bf16),
            pltpu.VMEM((rows, HEADS * QB), bf16),
            pltpu.VMEM((rows, HEADS * QB), bf16),
            pltpu.VMEM((rows, 1, QB, QB), jnp.int32),
            pltpu.VMEM((rows, 1, QB), f32),
            pltpu.VMEM((rows, 1, QB, QB), jnp.int32),
            pltpu.VMEM((rows, 1, QB), f32),
            pltpu.SMEM((rows,), jnp.int32),
            pltpu.VMEM((TENSORS, 10, QB), bf16),
            pltpu.VMEM((NZ * NX, 10, QB), bf16),
            pltpu.VMEM((160, QB), f32),
            pltpu.VMEM((depth, QB), bf16),
            pltpu.VMEM((640, QB), bf16),
            pltpu.VMEM((128, QB), f32),
            pltpu.VMEM((128, QB), f32),
            pltpu.VMEM((128, QB), f32),
            pltpu.VMEM((128, QB), f32),
            pltpu.VMEM((HEADS + 1, rows, QB), f32),
            pltpu.VMEM((HEADS + 1, rows, QB), f32),
            pltpu.VMEM((rows, QB), bf16),
            pltpu.VMEM((rows, QB), bf16),
            dma((8,)),
            dma((NZ * NX,)),
            dma((NZ * NX,)),
            dma((2, 4, 2)),
            dma((2, 4, 2)),
            dma((9,)),
            dma((9,)),
            dma((3,)),
            dma((3,)),
        ],
        compiler_params=pltpu.CompilerParams(
            collective_id=0, has_side_effects=True, vmem_limit_bytes=62000000
        ),
        cost_estimate=pl.CostEstimate(flops=60000000, bytes_accessed=6000000, transcendentals=100000),
        name="sync_decode",
    )(*args)
    synced, scales, attended = pl.pallas_call(
        settle,
        out_shape=(
            jax.ShapeDtypeStruct((depth, QB), bf16),
            jax.ShapeDtypeStruct((1, depth // QB), f32),
            jax.ShapeDtypeStruct((rows, HEADS * QB), bf16),
        ),
        in_specs=[vmem] * 3,
        out_specs=(hbm,) * 3,
        scratch_shapes=[dma((PARTS + 2,))],
        compiler_params=pltpu.CompilerParams(vmem_limit_bytes=8 * 1024 * 1024),
        name="settle",
    )(synced, scales, attended)
    return synced, scales.reshape(depth // QB, 1), attended


def solution(mesh):
    placed = (
        P(("replica", "tensor"), None),
        P("replica", None),
        P("replica", "tensor"),
        P("replica", "tensor", None, None),
        P("replica", "tensor", None),
        P("replica", "tensor", None, None),
        P("replica", "tensor", None),
        P("replica"),
    )
    return jax.shard_map(
        shards,
        mesh=mesh,
        in_specs=placed,
        out_specs=(P(None, "tensor"), P(None, "tensor"), P("replica", "tensor")),
        check_vma=False,
    )
```

```python
import math

import jax
import jax.numpy as jnp
from jax import lax
from jax.experimental import pallas as pl
from jax.experimental.pallas import tpu as pltpu
from jax.sharding import PartitionSpec as P

HEADS = 4
QB = 128
EPSILON = 1e-06
ROPE_BASE = 1000000.0
MASKED = -1e30
MESH = pl.DeviceIdType.MESH

NY = 8
NX = 4
NZ = 8
ZLO = 4
TENSORS = 16
LAST = 7


def kernel(
    w_hbm, hid_hbm, q_hbm, kc_hbm, ks_hbm, vc_hbm, vs_hbm, len_hbm,
    synced_out, scale_out, att_out,
    w_v, hid_v, q_v, pq_v, kc_v, ks_v, vc_v, vs_v, len_s,
    stage, landed, packed, gathered, group, scale_v,
    qs, osc, mlsc, psend, precv, esend, erecv,
    merged, load_sem, plane_send, plane_recv, row_send, ring_recv, sib_recv,
    pair_send, pair_recv,
):
    rep = lax.axis_index("replica")
    ten = lax.axis_index("tensor")
    y = rep // 4
    zhi = (rep // 2) % 2
    core = rep % 2
    half = ten % 2
    x = ten % NX
    z = zhi * ZLO + ten // NX

    def replica_of(yy, zz, cc):
        return (yy * 2 + zz) * 2 + cc

    def plane_id(zz, xx):
        return {"replica": replica_of(y, zz // ZLO, core), "tensor": (zz % ZLO) * NX + xx}

    def along_y(steps):
        return {"replica": replica_of((y + NY + steps) % NY, zhi, core), "tensor": ten}

    sib_id = {"replica": replica_of(y, zhi, 1 - core), "tensor": ten}
    pair_id = plane_id(z, x ^ 1)

    loads = [
        pltpu.make_async_copy(src, dst, load_sem.at[i])
        for i, (src, dst) in enumerate(
            (
                (w_hbm, w_v), (q_hbm, q_v), (kc_hbm, kc_v), (ks_hbm, ks_v), (len_hbm, len_s),
                (vc_hbm, vc_v), (vs_hbm, vs_v), (hid_hbm, hid_v),
            )
        )
    ]
    load_w, load_q, load_kc, load_ks, load_len, load_vc, load_vs, load_hid = loads
    load_w.start()
    load_q.start()

    barrier = pltpu.get_barrier_semaphore()
    peers = [
        plane_id((z + dz) % NZ, x ^ dx)
        for dz in (4, 3, 5, 2, 6, 1, 7, 0) for dx in (2, 3, 1, 0) if dz or dx
    ]
    peers += [along_y(2), along_y(-2), along_y(1), along_y(-1), sib_id]
    for other in peers:
        pl.semaphore_signal(barrier, inc=1, device_id=other, device_id_type=MESH)
    for copy in loads[2:]:
        copy.start()

    load_w.wait()
    for t in range(TENSORS):
        stage[t] = w_v[:, t * QB:(t + 1) * QB]
    load_q.wait()
    pl.semaphore_wait(barrier, len(peers))

    sends = []

    def launch(copy):
        copy.start()
        sends.append(copy)

    def pair_copy(i, src, dst):
        return pltpu.make_async_remote_copy(
            src_ref=src, dst_ref=dst, send_sem=pair_send.at[i], recv_sem=pair_recv.at[i],
            device_id=pair_id, device_id_type=MESH,
        )

    odd = z % 2
    offsets = ((2 + 4 * odd, 1, 7, 0), (6 - 4 * odd, 3, 5, 4))

    def plane_copy(part, dz, dx):
        to_z, to_x = (z + dz) % NZ, x ^ dx
        return pltpu.make_async_remote_copy(
            src_ref=stage.at[(to_z % ZLO) * NX + to_x], dst_ref=landed.at[z * NX + x],
            send_sem=plane_send, recv_sem=plane_recv.at[part],
            device_id=plane_id(to_z, to_x), device_id_type=MESH,
        )

    query_copy = pair_copy(0, q_v, pq_v)
    launch(query_copy)
    for part in range(2):
        for i, dz in enumerate(offsets[part]):
            for dx in (2, 3, 1, 0):
                if (part, i, dx) != (0, 3, 0):
                    plane_copy(part, dz, dx).start()
    landed[z * NX + x] = stage[ten]

    root = math.sqrt(QB)
    position = lax.broadcasted_iota(jnp.int32, (8, QB), 1) + half * QB
    lane = lax.broadcasted_iota(jnp.int32, (8, QB), 1)
    lane16 = lax.broadcasted_iota(jnp.int32, (16, QB), 1)

    def ready_queries():
        load_len.wait()
        load_kc.wait()
        load_ks.wait()
        for h in range(HEADS):
            qs[pl.ds(h, 16, stride=8), :] = q_v[:, h * QB:(h + 1) * QB].astype(jnp.float32)
        query_copy.wait_recv()
        for h in range(HEADS):
            qs[pl.ds(HEADS + h, 16, stride=8), :] = pq_v[:, h * QB:(h + 1) * QB].astype(jnp.float32)
        load_vc.wait()
        load_vs.wait()

    def attend(first, last):
        for r in range(first, last):
            q_r = qs[pl.ds(r * 8, 8), :].astype(jnp.bfloat16)
            k_r = kc_v[r, 0].astype(jnp.float32).astype(jnp.bfloat16)
            score = lax.dot_general(
                q_r, k_r, (((1,), (1,)), ((), ())), preferred_element_type=jnp.float32
            )
            score = score * (ks_v[r] * (1.0 / root))
            live = position < len_s[r]
            score = jnp.where(live, score, MASKED)
            peak = jnp.max(score, axis=1, keepdims=True)
            weight = jnp.where(live, jnp.exp(score - peak), 0.0)
            total = jnp.sum(weight, axis=1, keepdims=True)
            weight = weight * vs_v[r]
            high = weight.astype(jnp.bfloat16).astype(jnp.float32)
            both = jnp.concatenate([high, weight - high], axis=0).astype(jnp.bfloat16)
            v_r = vc_v[r, 0].astype(jnp.float32).astype(jnp.bfloat16)
            out = jnp.dot(both, v_r, preferred_element_type=jnp.float32)
            osc[pl.ds(r * 8, 8), :] = out[:8] + out[8:]
            mlsc[pl.ds(r * 8, 8), :] = jnp.where(lane < 64, peak, total)


    partial_copy = pair_copy(1, psend, precv)

    def send_partials():
        small = jnp.zeros((16, QB), jnp.float32)
        for h in range(HEADS):
            psend[h] = osc[pl.ds(HEADS + h, 16, stride=8), :]
            ml = mlsc[pl.ds(HEADS + h, 16, stride=8), :]
            here = lane16 // 32 == h
            first = (lane16 // 16) % 2 == 0
            small = jnp.where(here, jnp.where(first, ml[:, 0:1], ml[:, 64:65]), small)
        psend[HEADS] = small
        launch(partial_copy)

    near = z // 2
    pairs = (near, (near + 3 + 2 * odd) % 4, (near + 1 + 2 * odd) % 4, (near + 2) % 4)

    def chunk(yy, cc, piece):
        base = (yy * 2 + cc) * 320 + (160 if piece == 1 else 0)
        return pl.ds(pl.multiple_of(base, 160), 320 if piece is None else 160)

    def origin_of(d, k):
        return (y + NY - k) % NY if d == 0 else (y + k) % NY

    def ring_copy(piece, d, k):
        leg = 2 if k % 2 == 0 else 1
        ref = gathered.at[chunk(origin_of(d, k - leg), core, piece), :]
        return pltpu.make_async_remote_copy(
            src_ref=ref, dst_ref=ref,
            send_sem=row_send, recv_sem=ring_recv.at[d, k - 1, piece],
            device_id=along_y(leg if d == 0 else -leg), device_id_type=MESH,
        )

    def arrived(piece, d, k):
        leg = 2 if k % 2 == 0 else 1
        ref = gathered.at[chunk(origin_of(d, k), core, piece), :]
        pltpu.make_async_remote_copy(
            src_ref=ref, dst_ref=ref,
            send_sem=row_send, recv_sem=ring_recv.at[d, k - 1, piece],
            device_id=along_y(leg if d == 0 else -leg), device_id_type=MESH,
        ).wait_recv()

    def sib_copy(i, origin, piece, cc):
        ref = gathered.at[chunk(origin, cc, piece), :]
        return pltpu.make_async_remote_copy(
            src_ref=ref, dst_ref=ref, send_sem=row_send, recv_sem=sib_recv.at[i],
            device_id=sib_id, device_id_type=MESH,
        )

    def plane_wait(part):
        blocks = landed.at[pl.ds(0, 15 + part)]
        pltpu.make_async_copy(blocks, blocks, plane_recv.at[part]).wait()

    def start_piece(piece):
        for i in range(2):
            for side in range(2):
                for e in range(NX):
                    packed[pl.ds((2 * i + side) * 40 + e * 10, 10), :] = landed[
                        (2 * pairs[2 * piece + i] + side) * NX + e
                    ].astype(jnp.float32)
        gathered[chunk(y, core, piece), :] = packed[...].astype(jnp.bfloat16)
        for k in (2, 1):
            for d in range(2):
                ring_copy(piece, d, k).start()

    plane_wait(0)
    start_piece(0)
    plane_wait(1)
    start_piece(1)
    sib_copy(0, y, None, core).start()
    ready_queries()
    attend(0, 16)
    send_partials()

    row16 = lax.broadcasted_iota(jnp.int32, (16, QB), 0)
    length = jnp.zeros((16, QB), jnp.float32)
    for r in range(16):
        length = jnp.where(row16 == r, len_s[r].astype(jnp.float32), length)
    freq_index = (lane16 % 64).astype(jnp.float32)
    angle = length * jnp.exp(freq_index * (-math.log(ROPE_BASE) / 64.0))
    cosine = jnp.cos(angle)
    sine = jnp.where(lane16 < 64, -jnp.sin(angle), jnp.sin(angle))

    load_hid.wait()

    def process(i, origin, projected):
        if i == LAST:
            for piece in range(2):
                sib_copy(LAST + piece, origin, piece, 1 - core).wait_recv()
        else:
            sib_copy(i, origin, None, 1 - core).wait_recv()
        for cc in range(2):
            for q in range(4):
                to = (pairs[q] // 2) * 320 + cc * 160 + (pairs[q] % 2) * 80
                at = (origin * 2 + cc) * 320 + q * 80
                group[pl.ds(pl.multiple_of(to, 80), 80), :] = gathered[pl.ds(pl.multiple_of(at, 80), 80), :]
        base = pl.multiple_of(origin * 640, 640)
        for b in range(5):
            raw = group[pl.ds(b * QB, QB), :].astype(jnp.float32)
            scale = jnp.max(jnp.abs(raw), axis=(0, 1), keepdims=True) + EPSILON
            q = (raw * (1.0 / scale)).astype(jnp.bfloat16)
            synced_out[pl.ds(pl.multiple_of(base + b * QB, QB), QB), :] = q
            h = hid_v[:, pl.ds(pl.multiple_of(base + b * QB, QB), QB)]
            part = jnp.dot(h, q, preferred_element_type=jnp.float32)
            projected = projected + part * scale
            scale_v[pl.ds(origin * 5 + b, 1), :] = jnp.broadcast_to(scale, (1, QB))
        return projected

    def receive(piece, k):
        for d in (0, 1) if k < 4 else (1 - piece,):
            arrived(piece, d, k)
            if k == 2:
                if d == 1 - piece:
                    ring_copy(piece, d, 4).start()
                ring_copy(piece, d, 3).start()
        if k == 4:
            sib_copy(LAST + piece, origin_of(0, 4), piece, core).start()

    def share(k):
        for d in range(2):
            sib_copy(2 * k - 1 + d, origin_of(d, k), None, core).start()

    projected = jnp.zeros((16, QB), jnp.float32)
    receive(0, 2)
    receive(0, 1)
    receive(1, 2)
    share(2)
    receive(1, 1)
    share(1)
    projected = process(0, y, projected)
    receive(0, 3)
    for d in range(2):
        projected = process(3 + d, origin_of(d, 2), projected)
    receive(1, 3)
    share(3)
    for d in range(2):
        projected = process(1 + d, origin_of(d, 1), projected)
    receive(0, 4)
    receive(1, 4)
    for d in range(2):
        projected = process(5 + d, origin_of(d, 3), projected)

    partial_copy.wait_recv()
    for h in range(HEADS):
        own = osc[pl.ds(h, 16, stride=8), :]
        ml = mlsc[pl.ds(h, 16, stride=8), :]
        own_peak, own_total = ml[:, 0:1], ml[:, 64:65]
        peer_peak = precv[HEADS, :, 32 * h:32 * h + 1]
        peer_total = precv[HEADS, :, 32 * h + 16:32 * h + 17]
        joint = jnp.maximum(own_peak, peer_peak)
        own_factor = jnp.exp(own_peak - joint)
        peer_factor = jnp.exp(peer_peak - joint)
        merged[0, h] = jnp.broadcast_to(joint, (16, QB))
        merged[1, h] = jnp.broadcast_to(own_total * own_factor + peer_total * peer_factor, (16, QB))
        merged[2, h] = own * own_factor + precv[h] * peer_factor
    projected = process(LAST, origin_of(0, 4), projected)

    rotated = projected * cosine + pltpu.roll(projected, 64, 1) * sine
    esend[...] = jnp.where(half == 1, projected, rotated).astype(jnp.bfloat16)
    entry_copy = pair_copy(2, esend, erecv)
    entry_copy.start()
    scale_out[...] = jnp.transpose(scale_v[...], (1, 0))[0:1, 0:40]
    for copy in sends:
        copy.wait_send()
    blocks = landed.at[pl.ds(0, 31)]
    pltpu.make_async_copy(blocks, blocks, plane_send).wait()
    rows = gathered.at[pl.ds(0, 4800), :]
    pltpu.make_async_copy(rows, rows, row_send).wait()
    entry_copy.wait()
    own = esend[...].astype(jnp.float32)
    other = erecv[...].astype(jnp.float32)
    key = jnp.where(half == 1, other, own)
    value = jnp.where(half == 1, own, other)
    for h in range(HEADS):
        joint, total, weighted = merged[0, h], merged[1, h], merged[2, h]
        q_h = q_v[:, h * QB:(h + 1) * QB].astype(jnp.float32)
        score = jnp.sum(q_h * key, axis=1, keepdims=True) / root
        peak = jnp.maximum(joint, score)
        cached = jnp.exp(joint - peak)
        fresh = jnp.exp(score - peak)
        result = (weighted * cached + fresh * value) / (total * cached + fresh)
        att_out[:, h * QB:(h + 1) * QB] = result.astype(jnp.bfloat16)


PARTS = 4


def settle(synced, scales, attended, synced_out, scales_out, attended_out, sem):
    step = synced.shape[0] // PARTS
    legs = [(scales, scales_out), (attended, attended_out)]
    legs += [(ref.at[pl.ds(i * step, step), :], out.at[pl.ds(i * step, step), :])
             for ref, out in ((synced, synced_out),) for i in range(PARTS)]
    copies = [pltpu.make_async_copy(one, other, sem.at[i]) for i, (one, other) in enumerate(legs)]
    for copy in copies:
        copy.start()
    for copy in copies:
        copy.wait()


def shards(*args):
    rows, depth = args[1].shape
    bf16, f32 = jnp.bfloat16, jnp.float32
    hbm = pl.BlockSpec(memory_space=pltpu.HBM)
    vmem = pl.BlockSpec(memory_space=pltpu.VMEM)
    dma = pltpu.SemaphoreType.DMA
    synced, scales, attended = pl.pallas_call(
        kernel,
        out_shape=(
            pltpu.VMEM((depth, QB), bf16),
            pltpu.VMEM((1, depth // QB), f32),
            pltpu.VMEM((rows, HEADS * QB), bf16),
        ),
        in_specs=[hbm] * 8,
        out_specs=(vmem, vmem, vmem),
        scratch_shapes=[
            pltpu.VMEM((10, 2048), bf16),
            pltpu.VMEM((rows, depth), bf16),
            pltpu.VMEM((rows, HEADS * QB), bf16),
            pltpu.VMEM((rows, HEADS * QB), bf16),
            pltpu.VMEM((rows, 1, QB, QB), jnp.int32),
            pltpu.VMEM((rows, 1, QB), f32),
            pltpu.VMEM((rows, 1, QB, QB), jnp.int32),
            pltpu.VMEM((rows, 1, QB), f32),
            pltpu.SMEM((rows,), jnp.int32),
            pltpu.VMEM((TENSORS, 10, QB), bf16),
            pltpu.VMEM((NZ * NX, 10, QB), bf16),
            pltpu.VMEM((160, QB), f32),
            pltpu.VMEM((depth, QB), bf16),
            pltpu.VMEM((640, QB), bf16),
            pltpu.VMEM((128, QB), f32),
            pltpu.VMEM((128, QB), f32),
            pltpu.VMEM((128, QB), f32),
            pltpu.VMEM((128, QB), f32),
            pltpu.VMEM((HEADS + 1, rows, QB), f32),
            pltpu.VMEM((HEADS + 1, rows, QB), f32),
            pltpu.VMEM((rows, QB), bf16),
            pltpu.VMEM((rows, QB), bf16),
            pltpu.VMEM((3, HEADS, rows, QB), f32),
            dma((8,)),
            dma,
            dma((2,)),
            dma,
            dma((2, 4, 2)),
            dma((9,)),
            dma((3,)),
            dma((3,)),
        ],
        compiler_params=pltpu.CompilerParams(
            collective_id=0, has_side_effects=True, vmem_limit_bytes=62000000
        ),
        cost_estimate=pl.CostEstimate(flops=60000000, bytes_accessed=6000000, transcendentals=100000),
        name="sync_decode",
    )(*args)
    synced, scales, attended = pl.pallas_call(
        settle,
        out_shape=(
            jax.ShapeDtypeStruct((depth, QB), bf16),
            jax.ShapeDtypeStruct((1, depth // QB), f32),
            jax.ShapeDtypeStruct((rows, HEADS * QB), bf16),
        ),
        in_specs=[vmem] * 3,
        out_specs=(hbm,) * 3,
        scratch_shapes=[dma((PARTS + 2,))],
        compiler_params=pltpu.CompilerParams(vmem_limit_bytes=8 * 1024 * 1024),
        name="settle",
    )(synced, scales, attended)
    return synced, scales.reshape(depth // QB, 1), attended


def solution(mesh):
    placed = (
        P(("replica", "tensor"), None),
        P("replica", None),
        P("replica", "tensor"),
        P("replica", "tensor", None, None),
        P("replica", "tensor", None),
        P("replica", "tensor", None, None),
        P("replica", "tensor", None),
        P("replica"),
    )
    return jax.shard_map(
        shards,
        mesh=mesh,
        in_specs=placed,
        out_specs=(P(None, "tensor"), P(None, "tensor"), P("replica", "tensor")),
        check_vma=False,
    )
```

```python
import math

import jax
import jax.numpy as jnp
from jax import lax
from jax.experimental import pallas as pl
from jax.experimental.pallas import tpu as pltpu
from jax.sharding import PartitionSpec as P

HEADS = 4
QB = 128
EPSILON = 1e-06
ROPE_BASE = 1000000.0
MASKED = -1e30
MESH = pl.DeviceIdType.MESH

NY = 8
NX = 4
NZ = 8
ZLO = 4
TENSORS = 16
LAST = 7


def kernel(
    w_hbm, hid_hbm, q_hbm, kc_hbm, ks_hbm, vc_hbm, vs_hbm, len_hbm,
    synced_out, scale_out, att_out,
    w_v, hid_v, q_v, pq_v, kc_v, ks_v, vc_v, vs_v, len_s,
    stage, landed, packed, gathered, group, scale_v,
    qs, osc, mlsc, psend, precv, esend, erecv,
    merged, load_sem, plane_send, plane_recv, row_send, ring_recv, sib_recv,
    pair_send, pair_recv,
):
    rep = lax.axis_index("replica")
    ten = lax.axis_index("tensor")
    y = rep // 4
    zhi = (rep // 2) % 2
    core = rep % 2
    half = ten % 2
    x = ten % NX
    z = zhi * ZLO + ten // NX

    def replica_of(yy, zz, cc):
        return (yy * 2 + zz) * 2 + cc

    def plane_id(zz, xx):
        return {"replica": replica_of(y, zz // ZLO, core), "tensor": (zz % ZLO) * NX + xx}

    def along_y(steps):
        return {"replica": replica_of((y + NY + steps) % NY, zhi, core), "tensor": ten}

    sib_id = {"replica": replica_of(y, zhi, 1 - core), "tensor": ten}
    pair_id = plane_id(z, x ^ 1)

    loads = [
        pltpu.make_async_copy(src, dst, load_sem.at[i])
        for i, (src, dst) in enumerate(
            (
                (w_hbm, w_v), (q_hbm, q_v), (kc_hbm, kc_v), (ks_hbm, ks_v), (len_hbm, len_s),
                (vc_hbm, vc_v), (vs_hbm, vs_v), (hid_hbm, hid_v),
            )
        )
    ]
    load_w, load_q, load_kc, load_ks, load_len, load_vc, load_vs, load_hid = loads
    load_w.start()
    load_q.start()

    barrier = pltpu.get_barrier_semaphore()
    peers = [
        plane_id((z + dz) % NZ, x ^ dx)
        for dz in (4, 3, 5, 2, 6, 1, 7, 0) for dx in (2, 3, 1, 0) if dz or dx
    ]
    peers += [along_y(2), along_y(-2), along_y(1), along_y(-1), sib_id]
    for other in peers:
        pl.semaphore_signal(barrier, inc=1, device_id=other, device_id_type=MESH)
    for copy in loads[2:]:
        copy.start()

    load_w.wait()
    for t in range(TENSORS):
        stage[t] = w_v[:, t * QB:(t + 1) * QB]
    load_q.wait()
    pl.semaphore_wait(barrier, len(peers))

    sends = []

    def launch(copy):
        copy.start()
        sends.append(copy)

    def pair_copy(i, src, dst):
        return pltpu.make_async_remote_copy(
            src_ref=src, dst_ref=dst, send_sem=pair_send.at[i], recv_sem=pair_recv.at[i],
            device_id=pair_id, device_id_type=MESH,
        )

    odd = z % 2
    offsets = ((2 + 4 * odd, 1, 7, 0), (6 - 4 * odd, 3, 5, 4))

    def plane_copy(part, dz, dx):
        to_z, to_x = (z + dz) % NZ, x ^ dx
        return pltpu.make_async_remote_copy(
            src_ref=stage.at[(to_z % ZLO) * NX + to_x], dst_ref=landed.at[z * NX + x],
            send_sem=plane_send, recv_sem=plane_recv.at[part],
            device_id=plane_id(to_z, to_x), device_id_type=MESH,
        )

    query_copy = pair_copy(0, q_v, pq_v)
    launch(query_copy)
    for part in range(2):
        for i, dz in enumerate(offsets[part]):
            for dx in (2, 3, 1, 0):
                if (part, i, dx) != (0, 3, 0):
                    plane_copy(part, dz, dx).start()
    landed[z * NX + x] = stage[ten]

    root = math.sqrt(QB)
    position = lax.broadcasted_iota(jnp.int32, (8, QB), 1) + half * QB
    lane = lax.broadcasted_iota(jnp.int32, (8, QB), 1)
    lane16 = lax.broadcasted_iota(jnp.int32, (16, QB), 1)

    def ready_queries():
        load_len.wait()
        load_kc.wait()
        load_ks.wait()
        for h in range(HEADS):
            qs[pl.ds(h, 16, stride=8), :] = q_v[:, h * QB:(h + 1) * QB].astype(jnp.float32)
        query_copy.wait_recv()
        for h in range(HEADS):
            qs[pl.ds(HEADS + h, 16, stride=8), :] = pq_v[:, h * QB:(h + 1) * QB].astype(jnp.float32)
        load_vc.wait()
        load_vs.wait()

    def attend(first, last):
        for r in range(first, last):
            q_r = qs[pl.ds(r * 8, 8), :].astype(jnp.bfloat16)
            k_r = kc_v[r, 0].astype(jnp.float32).astype(jnp.bfloat16)
            score = lax.dot_general(
                q_r, k_r, (((1,), (1,)), ((), ())), preferred_element_type=jnp.float32
            )
            score = score * (ks_v[r] * (1.0 / root))
            live = position < len_s[r]
            score = jnp.where(live, score, MASKED)
            peak = jnp.max(score, axis=1, keepdims=True)
            weight = jnp.where(live, jnp.exp(score - peak), 0.0)
            total = jnp.sum(weight, axis=1, keepdims=True)
            weight = weight * vs_v[r]
            high = weight.astype(jnp.bfloat16).astype(jnp.float32)
            both = jnp.concatenate([high, weight - high], axis=0).astype(jnp.bfloat16)
            v_r = vc_v[r, 0].astype(jnp.float32).astype(jnp.bfloat16)
            out = jnp.dot(both, v_r, preferred_element_type=jnp.float32)
            osc[pl.ds(r * 8, 8), :] = out[:8] + out[8:]
            mlsc[pl.ds(r * 8, 8), :] = jnp.where(lane < 64, peak, total)


    partial_copy = pair_copy(1, psend, precv)

    def send_partials():
        small = jnp.zeros((16, QB), jnp.float32)
        for h in range(HEADS):
            psend[h] = osc[pl.ds(HEADS + h, 16, stride=8), :]
            ml = mlsc[pl.ds(HEADS + h, 16, stride=8), :]
            here = lane16 // 32 == h
            first = (lane16 // 16) % 2 == 0
            small = jnp.where(here, jnp.where(first, ml[:, 0:1], ml[:, 64:65]), small)
        psend[HEADS] = small
        launch(partial_copy)

    near = z // 2
    pairs = (near, (near + 3 + 2 * odd) % 4, (near + 1 + 2 * odd) % 4, (near + 2) % 4)

    def chunk(yy, cc, piece):
        base = (yy * 2 + cc) * 320 + (160 if piece == 1 else 0)
        return pl.ds(pl.multiple_of(base, 160), 320 if piece is None else 160)

    def origin_of(d, k):
        return (y + NY - k) % NY if d == 0 else (y + k) % NY

    def ring_copy(piece, d, k):
        leg = 2 if k % 2 == 0 else 1
        ref = gathered.at[chunk(origin_of(d, k - leg), core, piece), :]
        return pltpu.make_async_remote_copy(
            src_ref=ref, dst_ref=ref,
            send_sem=row_send, recv_sem=ring_recv.at[d, k - 1, piece or 0],
            device_id=along_y(leg if d == 0 else -leg), device_id_type=MESH,
        )

    def arrived(piece, d, k):
        leg = 2 if k % 2 == 0 else 1
        ref = gathered.at[chunk(origin_of(d, k), core, piece), :]
        pltpu.make_async_remote_copy(
            src_ref=ref, dst_ref=ref,
            send_sem=row_send, recv_sem=ring_recv.at[d, k - 1, piece or 0],
            device_id=along_y(leg if d == 0 else -leg), device_id_type=MESH,
        ).wait_recv()

    def sib_copy(i, origin, piece, cc):
        ref = gathered.at[chunk(origin, cc, piece), :]
        return pltpu.make_async_remote_copy(
            src_ref=ref, dst_ref=ref, send_sem=row_send, recv_sem=sib_recv.at[i],
            device_id=sib_id, device_id_type=MESH,
        )

    def plane_wait(part):
        blocks = landed.at[pl.ds(0, 15 + part)]
        pltpu.make_async_copy(blocks, blocks, plane_recv.at[part]).wait()

    def start_piece(piece):
        for i in range(2):
            for side in range(2):
                for e in range(NX):
                    packed[pl.ds((2 * i + side) * 40 + e * 10, 10), :] = landed[
                        (2 * pairs[2 * piece + i] + side) * NX + e
                    ].astype(jnp.float32)
        gathered[chunk(y, core, piece), :] = packed[...].astype(jnp.bfloat16)
        for d in range(2):
            ring_copy(piece, d, 2).start()

    plane_wait(0)
    start_piece(0)
    plane_wait(1)
    start_piece(1)
    for d in range(2):
        ring_copy(None, d, 1).start()
    sib_copy(0, y, None, core).start()
    ready_queries()
    attend(0, 16)
    send_partials()

    row16 = lax.broadcasted_iota(jnp.int32, (16, QB), 0)
    length = jnp.zeros((16, QB), jnp.float32)
    for r in range(16):
        length = jnp.where(row16 == r, len_s[r].astype(jnp.float32), length)
    freq_index = (lane16 % 64).astype(jnp.float32)
    angle = length * jnp.exp(freq_index * (-math.log(ROPE_BASE) / 64.0))
    cosine = jnp.cos(angle)
    sine = jnp.where(lane16 < 64, -jnp.sin(angle), jnp.sin(angle))

    load_hid.wait()

    def process(i, origin, projected):
        if i == LAST:
            for piece in range(2):
                sib_copy(LAST + piece, origin, piece, 1 - core).wait_recv()
        else:
            sib_copy(i, origin, None, 1 - core).wait_recv()
        for cc in range(2):
            for q in range(4):
                to = (pairs[q] // 2) * 320 + cc * 160 + (pairs[q] % 2) * 80
                at = (origin * 2 + cc) * 320 + q * 80
                group[pl.ds(pl.multiple_of(to, 80), 80), :] = gathered[pl.ds(pl.multiple_of(at, 80), 80), :]
        base = pl.multiple_of(origin * 640, 640)
        for b in range(5):
            raw = group[pl.ds(b * QB, QB), :].astype(jnp.float32)
            scale = jnp.max(jnp.abs(raw), axis=(0, 1), keepdims=True) + EPSILON
            q = (raw * (1.0 / scale)).astype(jnp.bfloat16)
            synced_out[pl.ds(pl.multiple_of(base + b * QB, QB), QB), :] = q
            h = hid_v[:, pl.ds(pl.multiple_of(base + b * QB, QB), QB)]
            part = jnp.dot(h, q, preferred_element_type=jnp.float32)
            projected = projected + part * scale
            scale_v[pl.ds(origin * 5 + b, 1), :] = jnp.broadcast_to(scale, (1, QB))
        return projected

    def receive(piece, k):
        for d in (0, 1) if k < 4 else (1 - piece,):
            arrived(piece, d, k)
            if k == 2:
                if d == 1 - piece:
                    ring_copy(piece, d, 4).start()
                ring_copy(piece, d, 3).start()
        if k == 4:
            sib_copy(LAST + piece, origin_of(0, 4), piece, core).start()

    def share(k):
        for d in range(2):
            sib_copy(2 * k - 1 + d, origin_of(d, k), None, core).start()

    projected = jnp.zeros((16, QB), jnp.float32)
    receive(0, 2)
    receive(1, 2)
    share(2)
    for d in range(2):
        arrived(None, d, 1)
    share(1)
    projected = process(0, y, projected)
    receive(0, 3)
    for d in range(2):
        projected = process(3 + d, origin_of(d, 2), projected)
    receive(1, 3)
    share(3)
    for d in range(2):
        projected = process(1 + d, origin_of(d, 1), projected)
    receive(0, 4)
    receive(1, 4)
    for d in range(2):
        projected = process(5 + d, origin_of(d, 3), projected)

    partial_copy.wait_recv()
    for h in range(HEADS):
        own = osc[pl.ds(h, 16, stride=8), :]
        ml = mlsc[pl.ds(h, 16, stride=8), :]
        own_peak, own_total = ml[:, 0:1], ml[:, 64:65]
        peer_peak = precv[HEADS, :, 32 * h:32 * h + 1]
        peer_total = precv[HEADS, :, 32 * h + 16:32 * h + 17]
        joint = jnp.maximum(own_peak, peer_peak)
        own_factor = jnp.exp(own_peak - joint)
        peer_factor = jnp.exp(peer_peak - joint)
        merged[0, h] = jnp.broadcast_to(joint, (16, QB))
        merged[1, h] = jnp.broadcast_to(own_total * own_factor + peer_total * peer_factor, (16, QB))
        merged[2, h] = own * own_factor + precv[h] * peer_factor
    projected = process(LAST, origin_of(0, 4), projected)

    rotated = projected * cosine + pltpu.roll(projected, 64, 1) * sine
    esend[...] = jnp.where(half == 1, projected, rotated).astype(jnp.bfloat16)
    entry_copy = pair_copy(2, esend, erecv)
    entry_copy.start()
    scale_out[...] = jnp.transpose(scale_v[...], (1, 0))[0:1, 0:40]
    for copy in sends:
        copy.wait_send()
    blocks = landed.at[pl.ds(0, 31)]
    pltpu.make_async_copy(blocks, blocks, plane_send).wait()
    rows = gathered.at[pl.ds(0, 4800), :]
    pltpu.make_async_copy(rows, rows, row_send).wait()
    entry_copy.wait()
    own = esend[...].astype(jnp.float32)
    other = erecv[...].astype(jnp.float32)
    key = jnp.where(half == 1, other, own)
    value = jnp.where(half == 1, own, other)
    for h in range(HEADS):
        joint, total, weighted = merged[0, h], merged[1, h], merged[2, h]
        q_h = q_v[:, h * QB:(h + 1) * QB].astype(jnp.float32)
        score = jnp.sum(q_h * key, axis=1, keepdims=True) / root
        peak = jnp.maximum(joint, score)
        cached = jnp.exp(joint - peak)
        fresh = jnp.exp(score - peak)
        result = (weighted * cached + fresh * value) / (total * cached + fresh)
        att_out[:, h * QB:(h + 1) * QB] = result.astype(jnp.bfloat16)


PARTS = 4


def settle(synced, scales, attended, synced_out, scales_out, attended_out, sem):
    step = synced.shape[0] // PARTS
    legs = [(scales, scales_out), (attended, attended_out)]
    legs += [(ref.at[pl.ds(i * step, step), :], out.at[pl.ds(i * step, step), :])
             for ref, out in ((synced, synced_out),) for i in range(PARTS)]
    copies = [pltpu.make_async_copy(one, other, sem.at[i]) for i, (one, other) in enumerate(legs)]
    for copy in copies:
        copy.start()
    for copy in copies:
        copy.wait()


def shards(*args):
    rows, depth = args[1].shape
    bf16, f32 = jnp.bfloat16, jnp.float32
    hbm = pl.BlockSpec(memory_space=pltpu.HBM)
    vmem = pl.BlockSpec(memory_space=pltpu.VMEM)
    dma = pltpu.SemaphoreType.DMA
    synced, scales, attended = pl.pallas_call(
        kernel,
        out_shape=(
            pltpu.VMEM((depth, QB), bf16),
            pltpu.VMEM((1, depth // QB), f32),
            pltpu.VMEM((rows, HEADS * QB), bf16),
        ),
        in_specs=[hbm] * 8,
        out_specs=(vmem, vmem, vmem),
        scratch_shapes=[
            pltpu.VMEM((10, 2048), bf16),
            pltpu.VMEM((rows, depth), bf16),
            pltpu.VMEM((rows, HEADS * QB), bf16),
            pltpu.VMEM((rows, HEADS * QB), bf16),
            pltpu.VMEM((rows, 1, QB, QB), jnp.int32),
            pltpu.VMEM((rows, 1, QB), f32),
            pltpu.VMEM((rows, 1, QB, QB), jnp.int32),
            pltpu.VMEM((rows, 1, QB), f32),
            pltpu.SMEM((rows,), jnp.int32),
            pltpu.VMEM((TENSORS, 10, QB), bf16),
            pltpu.VMEM((NZ * NX, 10, QB), bf16),
            pltpu.VMEM((160, QB), f32),
            pltpu.VMEM((depth, QB), bf16),
            pltpu.VMEM((640, QB), bf16),
            pltpu.VMEM((128, QB), f32),
            pltpu.VMEM((128, QB), f32),
            pltpu.VMEM((128, QB), f32),
            pltpu.VMEM((128, QB), f32),
            pltpu.VMEM((HEADS + 1, rows, QB), f32),
            pltpu.VMEM((HEADS + 1, rows, QB), f32),
            pltpu.VMEM((rows, QB), bf16),
            pltpu.VMEM((rows, QB), bf16),
            pltpu.VMEM((3, HEADS, rows, QB), f32),
            dma((8,)),
            dma,
            dma((2,)),
            dma,
            dma((2, 4, 2)),
            dma((9,)),
            dma((3,)),
            dma((3,)),
        ],
        compiler_params=pltpu.CompilerParams(
            collective_id=0, has_side_effects=True, vmem_limit_bytes=62000000
        ),
        cost_estimate=pl.CostEstimate(flops=60000000, bytes_accessed=6000000, transcendentals=100000),
        name="sync_decode",
    )(*args)
    synced, scales, attended = pl.pallas_call(
        settle,
        out_shape=(
            jax.ShapeDtypeStruct((depth, QB), bf16),
            jax.ShapeDtypeStruct((1, depth // QB), f32),
            jax.ShapeDtypeStruct((rows, HEADS * QB), bf16),
        ),
        in_specs=[vmem] * 3,
        out_specs=(hbm,) * 3,
        scratch_shapes=[dma((PARTS + 2,))],
        compiler_params=pltpu.CompilerParams(vmem_limit_bytes=8 * 1024 * 1024),
        name="settle",
    )(synced, scales, attended)
    return synced, scales.reshape(depth // QB, 1), attended


def solution(mesh):
    placed = (
        P(("replica", "tensor"), None),
        P("replica", None),
        P("replica", "tensor"),
        P("replica", "tensor", None, None),
        P("replica", "tensor", None),
        P("replica", "tensor", None, None),
        P("replica", "tensor", None),
        P("replica"),
    )
    return jax.shard_map(
        shards,
        mesh=mesh,
        in_specs=placed,
        out_specs=(P(None, "tensor"), P(None, "tensor"), P("replica", "tensor")),
        check_vma=False,
    )
```

```python
import math

import jax
import jax.numpy as jnp
from jax import lax
from jax.experimental import pallas as pl
from jax.experimental.pallas import tpu as pltpu
from jax.sharding import PartitionSpec as P

HEADS = 4
QB = 128
EPSILON = 1e-06
ROPE_BASE = 1000000.0
MASKED = -1e30
MESH = pl.DeviceIdType.MESH

NY = 8
NX = 4
NZ = 8
ZLO = 4
TENSORS = 16
LAST = 7


def kernel(
    w_hbm, hid_hbm, q_hbm, kc_hbm, ks_hbm, vc_hbm, vs_hbm, len_hbm,
    synced_out, scale_out, att_out,
    w_v, hid_v, q_v, pq_v, kc_v, ks_v, vc_v, vs_v, len_s,
    stage, landed, packed, gathered, group, scale_v,
    qs, osc, mlsc, psend, precv, esend, erecv,
    merged, load_sem, plane_send, plane_recv, row_send, ring_recv, sib_recv,
    pair_send, pair_recv,
):
    rep = lax.axis_index("replica")
    ten = lax.axis_index("tensor")
    y = rep // 4
    zhi = (rep // 2) % 2
    core = rep % 2
    half = ten % 2
    x = ten % NX
    z = zhi * ZLO + ten // NX

    def replica_of(yy, zz, cc):
        return (yy * 2 + zz) * 2 + cc

    def plane_id(zz, xx):
        return {"replica": replica_of(y, zz // ZLO, core), "tensor": (zz % ZLO) * NX + xx}

    def along_y(steps):
        return {"replica": replica_of((y + NY + steps) % NY, zhi, core), "tensor": ten}

    sib_id = {"replica": replica_of(y, zhi, 1 - core), "tensor": ten}
    pair_id = plane_id(z, x ^ 1)

    loads = [
        pltpu.make_async_copy(src, dst, load_sem.at[i])
        for i, (src, dst) in enumerate(
            (
                (w_hbm, w_v), (q_hbm, q_v), (kc_hbm, kc_v), (ks_hbm, ks_v), (len_hbm, len_s),
                (vc_hbm, vc_v), (vs_hbm, vs_v), (hid_hbm, hid_v),
            )
        )
    ]
    load_w, load_q, load_kc, load_ks, load_len, load_vc, load_vs, load_hid = loads
    load_w.start()
    load_q.start()

    barrier = pltpu.get_barrier_semaphore()
    peers = [
        plane_id((z + dz) % NZ, x ^ dx)
        for dz in (4, 3, 5, 2, 6, 1, 7, 0) for dx in (2, 3, 1, 0) if dz or dx
    ]
    peers += [along_y(2), along_y(-2), along_y(1), along_y(-1), sib_id]
    for other in peers:
        pl.semaphore_signal(barrier, inc=1, device_id=other, device_id_type=MESH)
    for copy in loads[2:]:
        copy.start()

    load_w.wait()
    for t in range(TENSORS):
        stage[t] = w_v[:, t * QB:(t + 1) * QB]
    load_q.wait()
    pl.semaphore_wait(barrier, len(peers))

    sends = []

    def launch(copy):
        copy.start()
        sends.append(copy)

    def pair_copy(i, src, dst):
        return pltpu.make_async_remote_copy(
            src_ref=src, dst_ref=dst, send_sem=pair_send.at[i], recv_sem=pair_recv.at[i],
            device_id=pair_id, device_id_type=MESH,
        )

    odd = z % 2
    offsets = ((2 + 4 * odd, 1, 7, 0), (6 - 4 * odd, 3, 5, 4))

    def plane_copy(part, dz, dx):
        to_z, to_x = (z + dz) % NZ, x ^ dx
        return pltpu.make_async_remote_copy(
            src_ref=stage.at[(to_z % ZLO) * NX + to_x], dst_ref=landed.at[z * NX + x],
            send_sem=plane_send, recv_sem=plane_recv.at[part],
            device_id=plane_id(to_z, to_x), device_id_type=MESH,
        )

    query_copy = pair_copy(0, q_v, pq_v)
    launch(query_copy)
    for part in range(2):
        for i, dz in enumerate(offsets[part]):
            for dx in (2, 3, 1, 0):
                if (part, i, dx) != (0, 3, 0):
                    plane_copy(part, dz, dx).start()
    landed[z * NX + x] = stage[ten]

    root = math.sqrt(QB)
    position = lax.broadcasted_iota(jnp.int32, (8, QB), 1) + half * QB
    lane = lax.broadcasted_iota(jnp.int32, (8, QB), 1)
    lane16 = lax.broadcasted_iota(jnp.int32, (16, QB), 1)

    def ready_queries():
        load_len.wait()
        load_kc.wait()
        load_ks.wait()
        for h in range(HEADS):
            qs[pl.ds(h, 16, stride=8), :] = q_v[:, h * QB:(h + 1) * QB].astype(jnp.float32)
        query_copy.wait_recv()
        for h in range(HEADS):
            qs[pl.ds(HEADS + h, 16, stride=8), :] = pq_v[:, h * QB:(h + 1) * QB].astype(jnp.float32)
        load_vc.wait()
        load_vs.wait()

    def attend(first, last):
        for r in range(first, last):
            q_r = qs[pl.ds(r * 8, 8), :].astype(jnp.bfloat16)
            k_r = kc_v[r, 0].astype(jnp.float32).astype(jnp.bfloat16)
            score = lax.dot_general(
                q_r, k_r, (((1,), (1,)), ((), ())), preferred_element_type=jnp.float32
            )
            score = score * (ks_v[r] * (1.0 / root))
            live = position < len_s[r]
            score = jnp.where(live, score, MASKED)
            peak = jnp.max(score, axis=1, keepdims=True)
            weight = jnp.where(live, jnp.exp(score - peak), 0.0)
            total = jnp.sum(weight, axis=1, keepdims=True)
            weight = weight * vs_v[r]
            high = weight.astype(jnp.bfloat16).astype(jnp.float32)
            both = jnp.concatenate([high, weight - high], axis=0).astype(jnp.bfloat16)
            v_r = vc_v[r, 0].astype(jnp.float32).astype(jnp.bfloat16)
            out = jnp.dot(both, v_r, preferred_element_type=jnp.float32)
            osc[pl.ds(r * 8, 8), :] = out[:8] + out[8:]
            mlsc[pl.ds(r * 8, 8), :] = jnp.where(lane < 64, peak, total)


    partial_copy = pair_copy(1, psend, precv)

    def send_partials():
        small = jnp.zeros((16, QB), jnp.float32)
        for h in range(HEADS):
            psend[h] = osc[pl.ds(HEADS + h, 16, stride=8), :]
            ml = mlsc[pl.ds(HEADS + h, 16, stride=8), :]
            here = lane16 // 32 == h
            first = (lane16 // 16) % 2 == 0
            small = jnp.where(here, jnp.where(first, ml[:, 0:1], ml[:, 64:65]), small)
        psend[HEADS] = small
        launch(partial_copy)

    near = z // 2
    pairs = (near, (near + 3 + 2 * odd) % 4, (near + 1 + 2 * odd) % 4, (near + 2) % 4)

    def chunk(yy, cc, piece):
        base = (yy * 2 + cc) * 320 + (160 if piece == 1 else 0)
        return pl.ds(pl.multiple_of(base, 160), 320 if piece is None else 160)

    def origin_of(d, k):
        return (y + NY - k) % NY if d == 0 else (y + k) % NY

    def ring_slot(piece, d, k):
        return {1: d, 3: 2 + d}[k] if k % 2 else {2: 4 + 2 * d, 4: 8}[k] + piece

    def ring_copy(piece, d, k):
        leg = 2 if k % 2 == 0 else 1
        ref = gathered.at[chunk(origin_of(d, k - leg), core, piece), :]
        return pltpu.make_async_remote_copy(
            src_ref=ref, dst_ref=ref,
            send_sem=row_send, recv_sem=ring_recv.at[ring_slot(piece, d, k)],
            device_id=along_y(leg if d == 0 else -leg), device_id_type=MESH,
        )

    def arrived(piece, d, k):
        leg = 2 if k % 2 == 0 else 1
        ref = gathered.at[chunk(origin_of(d, k), core, piece), :]
        pltpu.make_async_remote_copy(
            src_ref=ref, dst_ref=ref,
            send_sem=row_send, recv_sem=ring_recv.at[ring_slot(piece, d, k)],
            device_id=along_y(leg if d == 0 else -leg), device_id_type=MESH,
        ).wait_recv()

    def sib_copy(i, origin, piece, cc):
        ref = gathered.at[chunk(origin, cc, piece), :]
        return pltpu.make_async_remote_copy(
            src_ref=ref, dst_ref=ref, send_sem=row_send, recv_sem=sib_recv.at[i],
            device_id=sib_id, device_id_type=MESH,
        )

    def plane_wait(part):
        blocks = landed.at[pl.ds(0, 15 + part)]
        pltpu.make_async_copy(blocks, blocks, plane_recv.at[part]).wait()

    def start_piece(piece):
        for i in range(2):
            for side in range(2):
                for e in range(NX):
                    packed[pl.ds((2 * i + side) * 40 + e * 10, 10), :] = landed[
                        (2 * pairs[2 * piece + i] + side) * NX + e
                    ].astype(jnp.float32)
        gathered[chunk(y, core, piece), :] = packed[...].astype(jnp.bfloat16)
        for k in (2, 1):
            for d in range(2):
                ring_copy(piece, d, k).start()

    plane_wait(0)
    start_piece(0)
    plane_wait(1)
    start_piece(1)
    sib_copy(0, y, None, core).start()
    ready_queries()
    attend(0, 16)
    send_partials()

    row16 = lax.broadcasted_iota(jnp.int32, (16, QB), 0)
    length = jnp.zeros((16, QB), jnp.float32)
    for r in range(16):
        length = jnp.where(row16 == r, len_s[r].astype(jnp.float32), length)
    freq_index = (lane16 % 64).astype(jnp.float32)
    angle = length * jnp.exp(freq_index * (-math.log(ROPE_BASE) / 64.0))
    cosine = jnp.cos(angle)
    sine = jnp.where(lane16 < 64, -jnp.sin(angle), jnp.sin(angle))

    load_hid.wait()

    def process(i, origin, projected):
        if i == LAST:
            for piece in range(2):
                sib_copy(LAST + piece, origin, piece, 1 - core).wait_recv()
        else:
            sib_copy(i, origin, None, 1 - core).wait_recv()
        for cc in range(2):
            for q in range(4):
                to = (pairs[q] // 2) * 320 + cc * 160 + (pairs[q] % 2) * 80
                at = (origin * 2 + cc) * 320 + q * 80
                group[pl.ds(pl.multiple_of(to, 80), 80), :] = gathered[pl.ds(pl.multiple_of(at, 80), 80), :]
        base = pl.multiple_of(origin * 640, 640)
        for b in range(5):
            raw = group[pl.ds(b * QB, QB), :].astype(jnp.float32)
            scale = jnp.max(jnp.abs(raw), axis=(0, 1), keepdims=True) + EPSILON
            q = (raw * (1.0 / scale)).astype(jnp.bfloat16)
            synced_out[pl.ds(pl.multiple_of(base + b * QB, QB), QB), :] = q
            h = hid_v[:, pl.ds(pl.multiple_of(base + b * QB, QB), QB)]
            part = jnp.dot(h, q, preferred_element_type=jnp.float32)
            projected = projected + part * scale
            scale_v[pl.ds(origin * 5 + b, 1), :] = jnp.broadcast_to(scale, (1, QB))
        return projected

    def receive(piece, k):
        for d in (0, 1) if k < 4 else (1 - piece,):
            arrived(piece, d, k)
            if k == 2:
                if d == 1 - piece:
                    ring_copy(piece, d, 4).start()
                ring_copy(piece, d, 3).start()
        if k == 4:
            sib_copy(LAST + piece, origin_of(0, 4), piece, core).start()

    def share(k):
        for d in range(2):
            sib_copy(2 * k - 1 + d, origin_of(d, k), None, core).start()

    projected = jnp.zeros((16, QB), jnp.float32)
    receive(0, 2)
    receive(1, 2)
    share(2)
    for d in range(2):
        arrived(None, d, 1)
    share(1)
    projected = process(0, y, projected)
    for d in range(2):
        projected = process(3 + d, origin_of(d, 2), projected)
    for d in range(2):
        arrived(None, d, 3)
    share(3)
    for d in range(2):
        projected = process(1 + d, origin_of(d, 1), projected)
    receive(0, 4)
    receive(1, 4)
    for d in range(2):
        projected = process(5 + d, origin_of(d, 3), projected)

    partial_copy.wait_recv()
    for h in range(HEADS):
        own = osc[pl.ds(h, 16, stride=8), :]
        ml = mlsc[pl.ds(h, 16, stride=8), :]
        own_peak, own_total = ml[:, 0:1], ml[:, 64:65]
        peer_peak = precv[HEADS, :, 32 * h:32 * h + 1]
        peer_total = precv[HEADS, :, 32 * h + 16:32 * h + 17]
        joint = jnp.maximum(own_peak, peer_peak)
        own_factor = jnp.exp(own_peak - joint)
        peer_factor = jnp.exp(peer_peak - joint)
        merged[0, h] = jnp.broadcast_to(joint, (16, QB))
        merged[1, h] = jnp.broadcast_to(own_total * own_factor + peer_total * peer_factor, (16, QB))
        merged[2, h] = own * own_factor + precv[h] * peer_factor
    projected = process(LAST, origin_of(0, 4), projected)

    rotated = projected * cosine + pltpu.roll(projected, 64, 1) * sine
    esend[...] = jnp.where(half == 1, projected, rotated).astype(jnp.bfloat16)
    entry_copy = pair_copy(2, esend, erecv)
    entry_copy.start()
    scale_out[...] = jnp.transpose(scale_v[...], (1, 0))[0:1, 0:40]
    for copy in sends:
        copy.wait_send()
    blocks = landed.at[pl.ds(0, 31)]
    pltpu.make_async_copy(blocks, blocks, plane_send).wait()
    rows = gathered.at[pl.ds(0, 4800), :]
    pltpu.make_async_copy(rows, rows, row_send).wait()
    entry_copy.wait()
    own = esend[...].astype(jnp.float32)
    other = erecv[...].astype(jnp.float32)
    key = jnp.where(half == 1, other, own)
    value = jnp.where(half == 1, own, other)
    for h in range(HEADS):
        joint, total, weighted = merged[0, h], merged[1, h], merged[2, h]
        q_h = q_v[:, h * QB:(h + 1) * QB].astype(jnp.float32)
        score = jnp.sum(q_h * key, axis=1, keepdims=True) / root
        peak = jnp.maximum(joint, score)
        cached = jnp.exp(joint - peak)
        fresh = jnp.exp(score - peak)
        result = (weighted * cached + fresh * value) / (total * cached + fresh)
        att_out[:, h * QB:(h + 1) * QB] = result.astype(jnp.bfloat16)


PARTS = 4


def settle(synced, scales, attended, synced_out, scales_out, attended_out, sem):
    step = synced.shape[0] // PARTS
    legs = [(scales, scales_out), (attended, attended_out)]
    legs += [(ref.at[pl.ds(i * step, step), :], out.at[pl.ds(i * step, step), :])
             for ref, out in ((synced, synced_out),) for i in range(PARTS)]
    copies = [pltpu.make_async_copy(one, other, sem.at[i]) for i, (one, other) in enumerate(legs)]
    for copy in copies:
        copy.start()
    for copy in copies:
        copy.wait()


def shards(*args):
    rows, depth = args[1].shape
    bf16, f32 = jnp.bfloat16, jnp.float32
    hbm = pl.BlockSpec(memory_space=pltpu.HBM)
    vmem = pl.BlockSpec(memory_space=pltpu.VMEM)
    dma = pltpu.SemaphoreType.DMA
    synced, scales, attended = pl.pallas_call(
        kernel,
        out_shape=(
            pltpu.VMEM((depth, QB), bf16),
            pltpu.VMEM((1, depth // QB), f32),
            pltpu.VMEM((rows, HEADS * QB), bf16),
        ),
        in_specs=[hbm] * 8,
        out_specs=(vmem, vmem, vmem),
        scratch_shapes=[
            pltpu.VMEM((10, 2048), bf16),
            pltpu.VMEM((rows, depth), bf16),
            pltpu.VMEM((rows, HEADS * QB), bf16),
            pltpu.VMEM((rows, HEADS * QB), bf16),
            pltpu.VMEM((rows, 1, QB, QB), jnp.int32),
            pltpu.VMEM((rows, 1, QB), f32),
            pltpu.VMEM((rows, 1, QB, QB), jnp.int32),
            pltpu.VMEM((rows, 1, QB), f32),
            pltpu.SMEM((rows,), jnp.int32),
            pltpu.VMEM((TENSORS, 10, QB), bf16),
            pltpu.VMEM((NZ * NX, 10, QB), bf16),
            pltpu.VMEM((160, QB), f32),
            pltpu.VMEM((depth, QB), bf16),
            pltpu.VMEM((640, QB), bf16),
            pltpu.VMEM((128, QB), f32),
            pltpu.VMEM((128, QB), f32),
            pltpu.VMEM((128, QB), f32),
            pltpu.VMEM((128, QB), f32),
            pltpu.VMEM((HEADS + 1, rows, QB), f32),
            pltpu.VMEM((HEADS + 1, rows, QB), f32),
            pltpu.VMEM((rows, QB), bf16),
            pltpu.VMEM((rows, QB), bf16),
            pltpu.VMEM((3, HEADS, rows, QB), f32),
            dma((8,)),
            dma,
            dma((2,)),
            dma,
            dma((10,)),
            dma((9,)),
            dma((3,)),
            dma((3,)),
        ],
        compiler_params=pltpu.CompilerParams(
            collective_id=0, has_side_effects=True, vmem_limit_bytes=62000000
        ),
        cost_estimate=pl.CostEstimate(flops=60000000, bytes_accessed=6000000, transcendentals=100000),
        name="sync_decode",
    )(*args)
    synced, scales, attended = pl.pallas_call(
        settle,
        out_shape=(
            jax.ShapeDtypeStruct((depth, QB), bf16),
            jax.ShapeDtypeStruct((1, depth // QB), f32),
            jax.ShapeDtypeStruct((rows, HEADS * QB), bf16),
        ),
        in_specs=[vmem] * 3,
        out_specs=(hbm,) * 3,
        scratch_shapes=[dma((PARTS + 2,))],
        compiler_params=pltpu.CompilerParams(vmem_limit_bytes=8 * 1024 * 1024),
        name="settle",
    )(synced, scales, attended)
    return synced, scales.reshape(depth // QB, 1), attended


def solution(mesh):
    placed = (
        P(("replica", "tensor"), None),
        P("replica", None),
        P("replica", "tensor"),
        P("replica", "tensor", None, None),
        P("replica", "tensor", None),
        P("replica", "tensor", None, None),
        P("replica", "tensor", None),
        P("replica"),
    )
    return jax.shard_map(
        shards,
        mesh=mesh,
        in_specs=placed,
        out_specs=(P(None, "tensor"), P(None, "tensor"), P("replica", "tensor")),
        check_vma=False,
    )
```
